128 devices in a mesh: row: 8 (over y, core), col: 16 (over x, z).
Axes of the slice: x: 4, y: 4, z: 4, core: 2. Of those that a mesh axis runs over, the one named last changes fastest.
Arguments:
- inputs: bfloat16 [2048, 8192], P('col', 'row'), may hold values from -6 to 6
- grad_out: bfloat16 [2048, 8192], P('col', 'row'), may hold values from -0.59765625 to 0.59765625
- gate_pre: bfloat16 [2048, 14336], P('row', 'col'), may hold values from -9 to 9
- up_pre: bfloat16 [2048, 14336], P('row', 'col'), may hold values from -6 to 6
- w_gate: bfloat16 [8192, 14336], P('row', 'col'), may hold values from -0.125 to 0.125
- w_up: bfloat16 [8192, 14336], P('row', 'col'), may hold values from -0.125 to 0.125
- w_down: bfloat16 [14336, 8192], P('col', 'row'), may hold values from -0.09375 to 0.09375
- mask_gate: int32 [64, 112], P('row', 'col'), may hold values 0 or 1
- mask_up: int32 [64, 112], P('row', 'col'), may hold values 0 or 1
- mask_down: int32 [112, 64], P('col', 'row'), may hold values 0 or 1
Outputs:
- grad_inputs: bfloat16 [2048, 8192], P('col', 'row')
- grad_gate: bfloat16 [8192, 14336], P('row', 'col')
- grad_up: bfloat16 [8192, 14336], P('row', 'col')
- grad_down: bfloat16 [14336, 8192], P('col', 'row')
The draws below stay inside these ranges and needn't reach their ends.
All inputs are finite; a program needn't handle non-finite values. No bound on the sum of `mask_gate` or of `mask_up` or of `mask_down` on one device may be relied on, other than what follows from the above.
Results may differ from the reference program's by a relative error of at most 0.005.
Values may be sent and summed in bfloat16 or wider, within the bound.
A program may use at most 128 MiB of HBM per device.

```python
import jax
import jax.numpy as jnp
from jax import lax

D = 8192
FF = 14336
BLK = 128
TOKENS = 2048


def with_ends(values, key, least, top_value):
    shape = values.shape
    index_at = [jax.random.randint(jax.random.fold_in(key, axis), (), 0, shape[axis]) for axis in range(len(shape))]
    values = values.at[tuple(index_at)].set(least)
    longest = shape.index(max(shape))
    index_at[longest] = (index_at[longest] + 1) % shape[longest]
    return values.at[tuple(index_at)].set(top_value)


def block_levels(stream_key, dims, split, smallest, high):
    factor_of = 1.0
    for axis_at, blocks in split:
        heights = jax.random.uniform(jax.random.fold_in(jax.random.fold_in(stream_key, 6), axis_at), (blocks,), jnp.float32, smallest / len(split), high / len(split))
        factor_of = factor_of * jnp.repeat(jnp.exp(heights), dims[axis_at] // blocks).reshape((-1,) + (1,) * (len(dims) - 1 - axis_at))
    return factor_of


def gaussian(own_key, dims, width, limit, shards=(), kind=jnp.bfloat16):
    level = block_levels(own_key, dims, shards, -0.22, 0.18) if shards else 1.0
    array = jax.random.normal(own_key, dims, jnp.float32) * width * level
    return jnp.minimum(jnp.maximum(array, -limit), limit).astype(kind)


def setup_inputs(seed: int = 0) -> dict:
    splits = jax.random.split(jax.random.key(seed), 11)
    return {
        "inputs": gaussian(splits[0], (TOKENS, D), 1.0, 6.0, ((0, 16), (1, 8))),
        "grad_out": gaussian(splits[1], (TOKENS, D), 0.1, 0.59765625, ((0, 16), (1, 8))),
        "gate_pre": gaussian(splits[2], (TOKENS, FF), 1.5, 9.0, ((0, 8), (1, 16))),
        "up_pre": gaussian(splits[3], (TOKENS, FF), 1.0, 6.0, ((0, 8), (1, 16))),
        "w_gate": gaussian(splits[4], (D, FF), (3 * D // 10) ** -0.5, 0.125, ((0, 8), (1, 16))),
        "w_up": gaussian(splits[5], (D, FF), (3 * D // 10) ** -0.5, 0.125, ((0, 8), (1, 16))),
        "w_down": gaussian(splits[6], (FF, D), (3 * FF // 10) ** -0.5, 0.09375, ((0, 16), (1, 8))),
        "mask_gate": with_ends((jax.random.randint(splits[7], (D // BLK, FF // BLK), 0, 10) < 3).astype(jnp.int32), jax.random.fold_in(splits[7], 1), 0, 1),
        "mask_up": with_ends((jax.random.randint(splits[8], (D // BLK, FF // BLK), 0, 10) < 3).astype(jnp.int32), jax.random.fold_in(splits[8], 1), 0, 1),
        "mask_down": with_ends((jax.random.randint(splits[9], (FF // BLK, D // BLK), 0, 10) < 3).astype(jnp.int32), jax.random.fold_in(splits[9], 1), 0, 1),
    }


def expand(mask):
    return jnp.repeat(jnp.repeat(mask, BLK, 0), BLK, 1).astype(jnp.bfloat16)


def reference(inputs, grad_out, gate_pre, up_pre, w_gate, w_up, w_down, mask_gate, mask_up, mask_down):
    keep_gate = expand(mask_gate)
    keep_up = expand(mask_up)
    keep_down = expand(mask_down)
    gate_eff = w_gate * keep_gate
    up_eff = w_up * keep_up
    down_eff = w_down * keep_down
    hidden_grad = lax.dot_general(grad_out, down_eff, (((1,), (1,)), ((), ())), preferred_element_type=jnp.float32)
    gated = gate_pre.astype(jnp.float32)
    upper = up_pre.astype(jnp.float32)
    sigma = jax.nn.sigmoid(gated)
    act = (gated * sigma * upper).astype(jnp.bfloat16)
    grad_g = (hidden_grad * upper * sigma * (1.0 + gated * (1.0 - sigma))).astype(jnp.bfloat16)
    grad_u = (hidden_grad * gated * sigma).astype(jnp.bfloat16)
    contract = (((1,), (1,)), ((), ()))
    grad_inputs = lax.dot_general(grad_g, gate_eff, contract, preferred_element_type=jnp.float32)
    grad_inputs = grad_inputs + lax.dot_general(grad_u, up_eff, contract, preferred_element_type=jnp.float32)
    tokens_dim = (((0,), (0,)), ((), ()))
    grad_gate = lax.dot_general(inputs, grad_g, tokens_dim, preferred_element_type=jnp.float32) * keep_gate.astype(jnp.float32)
    grad_up = lax.dot_general(inputs, grad_u, tokens_dim, preferred_element_type=jnp.float32) * keep_up.astype(jnp.float32)
    grad_down = lax.dot_general(act, grad_out, tokens_dim, preferred_element_type=jnp.float32) * keep_down.astype(jnp.float32)
    return (grad_inputs.astype(jnp.bfloat16), grad_gate.astype(jnp.bfloat16), grad_up.astype(jnp.bfloat16), grad_down.astype(jnp.bfloat16))
```

```python
import jax
import jax.numpy as jnp
from jax import lax
from jax.experimental import pallas as pl
from jax.experimental.pallas import tpu as pltpu
from jax.sharding import PartitionSpec as P

MESH = pl.DeviceIdType.MESH
BF = jnp.bfloat16
F32 = jnp.float32
NT = (((1,), (1,)), ((), ()))
TN = (((0,), (0,)), ((), ()))
RELS = (2, 1, -1, 0)
GROUPS = (0, 1, -1, 2)


def m4(value):
    return lax.rem(value + 8, 4)


def coords():
    row, col = lax.axis_index("row"), lax.axis_index("col")
    return lax.div(row, 2), lax.rem(row, 2), lax.div(col, 4), lax.rem(col, 4)


def device(y, k, x, z):
    return {"row": y * 2 + k, "col": x * 4 + z}


def remote(src, dst, send, recv, to):
    return pltpu.make_async_remote_copy(
        src_ref=src, dst_ref=dst, send_sem=send, recv_sem=recv, device_id=to, device_id_type=MESH
    )


class ColGather:
    def __init__(self, full, send, recv):
        self.full, self.send_sem, self.recv_sem = full, send, recv
        self.y, self.k, self.x, self.z = coords()

    def piece(self, q, c):
        return self.full.at[c, pl.ds(pl.multiple_of(q * 32, 32), 32)]

    def index(self, q, a, b):
        late = lax.div(q, 2)
        return m4(self.x + a * (1 - late) + b * late) * 4 + m4(self.z + a * late + b * (1 - late))

    def send(self, q, a, b, second, d, slot):
        c = self.index(q, a, b)
        late = lax.div(q, 2)
        along_z = late + second - 2 * late * second
        to = device(self.y, self.k, m4(self.x + d * (1 - along_z)), m4(self.z + d * along_z))
        remote(
            self.piece(q, c), self.piece(q, c), self.send_sem.at[q * 15 + slot], self.recv_sem.at[q, c], to
        ).start()

    def recv(self, q, a, b):
        c = self.index(q, a, b)
        remote(
            self.piece(q, c),
            self.piece(q, c),
            self.send_sem.at[0],
            self.recv_sem.at[q, c],
            device(self.y, self.k, m4(self.x + 1), self.z),
        ).wait_recv()

    def each(self, body):
        def step(q, carry):
            body(q, 1 - 2 * lax.rem(q, 2))
            return carry

        lax.fori_loop(0, 4, step, 0)

    def start(self):
        def own(q, w):
            self.send(q, 0, 0, 0, 1, 0)
            self.send(q, 0, 0, 0, -1, 1)

        def own_second(q, w):
            self.send(q, 0, 0, 1, 1, 2)
            self.send(q, 0, 0, 1, -1, 3)

        self.each(own)
        self.each(own_second)

    def steps(self):
        def first(q, w):
            self.recv(q, -w, 0)
            self.send(q, -w, 0, 0, w, 4)
            self.send(q, -w, 0, 1, 1, 5)
            self.send(q, -w, 0, 1, -1, 6)

        def second(q, w):
            self.recv(q, w, 0)
            self.send(q, w, 0, 1, 1, 7)
            self.send(q, w, 0, 1, -1, 8)

        def own_line(q, w):
            self.recv(q, 0, -w)
            self.send(q, 0, -w, 1, w, 9)

        def far(q, w):
            self.recv(q, 2, 0)
            self.send(q, 2, 0, 1, 1, 10)
            self.send(q, 2, 0, 1, -1, 11)

        for body in (first, second, own_line, far):
            self.each(body)
            yield
        for slot, a in ((12, -1), (13, 1), (14, 2)):

            def line(q, w, a=a, slot=slot):
                self.recv(q, a * w, -w)
                self.send(q, a * w, -w, 1, w, slot)

            self.each(line)
            yield
        for a in (0, -1, 1, 2):

            def last(q, w, a=a):
                self.recv(q, a * w, w)
                self.recv(q, a * w, 2)

            self.each(last)
            yield

    def finish(self):
        def one(i, carry):
            remote(
                self.piece(0, 0),
                self.piece(0, 0),
                self.send_sem.at[i],
                self.recv_sem.at[0, 0],
                device(self.y, self.k, m4(self.x + 1), self.z),
            ).wait_send()
            return carry

        lax.fori_loop(0, 60, one, 0)


class RowGather:
    def __init__(self, view, send, recv):
        self.view, self.send_sem, self.recv_sem = view, send, recv
        self.y, self.k, self.x, self.z = coords()

    def row(self, dy, sibling=False):
        return m4(self.y + dy) * 2 + (1 - self.k if sibling else self.k)

    def sibling(self):
        return device(self.y, 1 - self.k, self.x, self.z)

    def copy(self, h, r, slot, to):
        return remote(self.view(r, h), self.view(r, h), self.send_sem.at[h * 7 + slot], self.recv_sem.at[h, r], to)

    def ring(self, h, dy, d, slot):
        to = device(m4(self.y + d), self.k, self.x, self.z)
        self.copy(h, self.row(dy), slot, to).start()

    def cross(self, h, dy, slot):
        self.copy(h, self.row(dy), slot, self.sibling()).start()

    def recv(self, h, dy, sibling=False):
        self.copy(h, self.row(dy, sibling), 0, self.sibling()).wait_recv()

    def start_half(self, h):
        self.ring(h, 0, 1, 0)
        self.ring(h, 0, -1, 1)
        self.cross(h, 0, 2)

    def start(self):
        for h in (0, 1):
            self.start_half(h)

    def near(self):
        for h in (0, 1):
            w = 1 - 2 * h
            self.recv(h, -w)
            self.ring(h, -w, w, 3)
            self.cross(h, -w, 4)

    def other(self):
        for h in (0, 1):
            w = 1 - 2 * h
            self.recv(h, w)
            self.cross(h, w, 5)

    def far(self):
        for h in (0, 1):
            self.recv(h, 2)
            self.cross(h, 2, 6)

    def from_sibling(self, dy):
        for h in (0, 1):
            self.recv(h, dy, True)

    def finish(self):
        for h in (0, 1):
            for slot in range(7):
                self.copy(h, 0, slot, self.sibling()).wait_send()


def kernel(
    x_in, dy_in, g_in, u_in, wg_in, wu_in, wd_in, mg, mu, md,
    gi_out, gg_out, gu_out, gd_out,
    dy, xx, ga, ua, hd, act, wg, wu, wd, hp, rb, ys, yr, s1, r1, s2, r2, gi, stage,
    lsem, osem, col_s, col_r, row_s, row_r, sib_s, sib_r, ring_s, ring_r, gs, gr,
):
    y, k, x, z = coords()
    me_col, me_row = x * 4 + z, y * 2 + k
    sibling = device(y, 1 - k, x, z)
    up_y, down_y = device(m4(y + 1), k, x, z), device(m4(y - 1), k, x, z)

    local = [
        pltpu.make_async_copy(dy_in, dy.at[me_col], lsem.at[0]),
        pltpu.make_async_copy(g_in.at[pl.ds(0, 128)], ga.at[2 * me_row], lsem.at[1]),
        pltpu.make_async_copy(g_in.at[pl.ds(128, 128)], ga.at[2 * me_row + 1], lsem.at[2]),
        pltpu.make_async_copy(u_in.at[pl.ds(0, 128)], ua.at[2 * me_row], lsem.at[3]),
        pltpu.make_async_copy(u_in.at[pl.ds(128, 128)], ua.at[2 * me_row + 1], lsem.at[4]),
        pltpu.make_async_copy(wd_in, wd, lsem.at[5]),
        pltpu.make_async_copy(x_in, xx.at[me_col], lsem.at[6]),
        pltpu.make_async_copy(wg_in, wg, lsem.at[7]),
        pltpu.make_async_copy(wu_in, wu, lsem.at[8]),
    ]
    for copy in local:
        copy.start()

    barrier = pltpu.get_barrier_semaphore()
    for to in (
        device(y, k, m4(x + 1), z),
        device(y, k, m4(x - 1), z),
        device(y, k, x, m4(z + 1)),
        device(y, k, x, m4(z - 1)),
        up_y,
        down_y,
        sibling,
    ):
        pl.semaphore_signal(barrier, inc=1, device_id=to, device_id_type=MESH)
    pl.semaphore_wait(barrier, 7)

    dy_gather = ColGather(dy, col_s.at[0], col_r.at[0])
    x_gather = ColGather(xx, col_s.at[1], col_r.at[1])
    g_gather = RowGather(lambda r, h: ga.at[2 * r + h], row_s.at[0], row_r.at[0])
    u_gather = RowGather(lambda r, h: ua.at[2 * r + h], row_s.at[1], row_r.at[1])
    h_gather = RowGather(lambda r, h: hd.at[r, h], row_s.at[2], row_r.at[2])
    dy_steps, x_steps = dy_gather.steps(), x_gather.steps()

    def advance(steps, count):
        for _ in range(count):
            next(steps, None)

    def apply_mask(w, mask, rows, columns):
        def line(i, carry):
            here = pl.ds(pl.multiple_of(i * 128, 128), 128)
            for j in range(columns):
                keep = mask[i, j].astype(F32)
                block = w[here, j * 128 : (j + 1) * 128].astype(F32)
                w[here, j * 128 : (j + 1) * 128] = (block * keep).astype(BF)
            return carry

        lax.fori_loop(0, rows, line, 0)

    local[0].wait()
    dy_gather.start()
    for copy in local[1:5]:
        copy.wait()
    g_gather.start()
    u_gather.start()
    local[5].wait()
    apply_mask(wd, md, 7, 8)

    advance(dy_steps, 7)
    g_gather.near()
    local[6].wait()
    x_gather.start()
    advance(dy_steps, 4)
    u_gather.near()

    def across(slot):
        there = pl.ds(2 * (1 - k), 2)
        return remote(
            hp.at[slot, there, :, :, pl.ds(0, 896)], rb.at[slot], sib_s.at[slot], sib_r.at[slot], sibling
        )

    def partial(slot):
        j = m4(y + RELS[slot])
        rows = pl.ds(pl.multiple_of(j * 32, 32), 32)
        left = dy[:, rows, :].reshape(512, 1024)
        product = lax.dot_general(left, wd[...], NT, preferred_element_type=F32)
        hp[slot, :, :, :, 0:896] = product.reshape(4, 4, 32, 896)
        across(slot).start()

    def total(slot, h, i):
        return hp[slot, 2 * k + h, i, :, 0:896] + rb[slot, h, i]

    def ring_copy(n, to):
        return remote(ys.at[n], yr.at[n], ring_s.at[n], ring_r.at[n], to)

    def pack(n, slot, h, with_recv=None):
        def one(i, carry):
            value = total(slot, h, i)
            if with_recv is not None:
                value = value + yr[with_recv, i].astype(F32)
            ys[n, i] = value.astype(BF)
            return carry

        lax.fori_loop(0, 4, one, 0)

    partial(0)
    partial(1)
    across(0).wait_recv()
    pack(0, 0, 0)
    ring_copy(0, up_y).start()
    pack(1, 0, 1)
    ring_copy(1, down_y).start()
    partial(2)
    advance(x_steps, 1)
    across(1).wait_recv()
    pack(2, 1, 1)
    ring_copy(2, up_y).start()
    partial(3)
    across(2).wait_recv()
    pack(3, 2, 0)
    ring_copy(3, down_y).start()
    advance(x_steps, 1)

    local[7].wait()
    apply_mask(wg, mg, 8, 7)
    advance(x_steps, 1)
    g_gather.other()
    u_gather.other()
    local[8].wait()
    apply_mask(wu, mu, 8, 7)
    advance(x_steps, 1)
    g_gather.far()
    u_gather.far()
    advance(x_steps, 1)

    for offset in (0, 1, -1, 2):
        g_gather.from_sibling(offset)
        u_gather.from_sibling(offset)

    def activation(lo, hi):
        def one(c, carry):
            for part in range(4):
                rows = pl.ds(part * 32, 32)
                gated = ga[c, rows].astype(F32)
                act[c, rows] = (gated * jax.nn.sigmoid(gated) * ua[c, rows].astype(F32)).astype(BF)
            return carry

        lax.fori_loop(lo, hi, one, 0)

    activation(0, 8)
    advance(x_steps, 1)
    activation(8, 16)
    advance(x_steps, 1)

    ring_copy(0, up_y).wait_recv()
    pack(4, 1, 0, 0)
    ring_copy(4, up_y).start()
    ring_copy(1, up_y).wait_recv()
    pack(5, 2, 1, 1)
    ring_copy(5, down_y).start()

    outs = []

    def emit(slot, rows, columns, out, at):
        if len(outs) >= 4:
            outs[len(outs) - 4].wait()
        copy = pltpu.make_async_copy(
            stage.at[slot, pl.ds(0, rows), pl.ds(0, columns)], out.at[pl.ds(at, rows)], osem.at[slot]
        )
        return copy

    def weight_tile(left, right, mask, out, i, rows, columns):
        slot = len(outs) % 4
        copy = emit(slot, rows, columns, out, i * 256)
        a = left[:, :, i * 256 : i * 256 + rows].reshape(2048, rows)
        b = right[...].reshape(2048, columns)
        product = lax.dot_general(a, b, TN, preferred_element_type=F32)
        for p in range(rows // 128):
            for q in range(columns // 128):
                keep = mask[i * 2 + p, q].astype(F32)
                block = product[p * 128 : (p + 1) * 128, q * 128 : (q + 1) * 128]
                stage[slot, p * 128 : (p + 1) * 128, q * 128 : (q + 1) * 128] = (block * keep).astype(BF)
        copy.start()
        outs.append(copy)

    weight_tile(act, dy, md, gd_out, 0, 256, 1024)
    advance(x_steps, 1)
    weight_tile(act, dy, md, gd_out, 1, 256, 1024)
    advance(x_steps, 1)

    across(3).wait_recv()
    ring_copy(3, up_y).wait_recv()
    ring_copy(2, up_y).wait_recv()

    def finish_hidden(h, first, second):
        def one(i, carry):
            value = total(3, h, i) + yr[first, i].astype(F32) + yr[second, i].astype(F32)
            hd[me_row, h, i] = value.astype(BF)
            return carry

        lax.fori_loop(0, 4, one, 0)
        h_gather.start_half(h)

    ring_copy(4, up_y).wait_recv()
    finish_hidden(0, 4, 3)
    ring_copy(5, up_y).wait_recv()
    finish_hidden(1, 2, 5)
    for n in range(6):
        ring_copy(n, up_y).wait_send()
    for slot in range(4):
        across(slot).wait_send()
    g_gather.finish()
    u_gather.finish()

    def along(t, stage_at, d):
        if (t < 2) == (stage_at == 0):
            return device(y, k, x, m4(z + d))
        return device(y, k, m4(x + d), z)

    def group_copy(n, t, stage_at, kind):
        w = 1 - 2 * (t % 2)
        to = along(t, stage_at, -w if kind == 1 else w)
        at = n * 4 + t
        src, dst = (s1, r1) if stage_at == 0 else (s2, r2)
        return remote(
            src.at[at, kind], dst.at[at, kind], gs.at[at, stage_at, kind], gr.at[at, stage_at, kind], to
        )

    def columns(t):
        return pl.ds(t * 256, 256)

    def slab(n, t, d):
        if t < 2:
            return hp[n, :, m4(z + d), :, columns(t)]
        return hp[n, m4(x + d), :, :, columns(t)]

    def group_partial(n):
        j = m4(y + GROUPS[n])
        rows = pl.ds(pl.multiple_of(j * 32, 32), 32)

        def one(c, carry):
            gated = ga[c, rows].astype(F32)
            upper = ua[c, rows].astype(F32)
            hidden = hd[2 * j + lax.div(c, 8), lax.rem(lax.div(c, 4), 2), lax.rem(c, 4)].astype(F32)
            sigma = jax.nn.sigmoid(gated)
            ga[c, rows] = (hidden * upper * sigma * (1.0 + gated * (1.0 - sigma))).astype(BF)
            ua[c, rows] = (hidden * gated * sigma).astype(BF)
            return carry

        lax.fori_loop(0, 16, one, 0)
        product = lax.dot_general(ga[:, rows, :].reshape(512, 896), wg[...], NT, preferred_element_type=F32)
        product = product + lax.dot_general(
            ua[:, rows, :].reshape(512, 896), wu[...], NT, preferred_element_type=F32
        )
        hp[n] = product.reshape(4, 4, 32, 1024)
        for t in range(4):
            w = 1 - 2 * (t % 2)
            s1[n * 4 + t, 0] = slab(n, t, 2).astype(BF)
            group_copy(n, t, 0, 0).start()
        for t in range(4):
            w = 1 - 2 * (t % 2)
            s1[n * 4 + t, 1] = slab(n, t, -w).astype(BF)
            group_copy(n, t, 0, 1).start()

    def group_combine(n):
        for t in range(4):
            w = 1 - 2 * (t % 2)
            at = n * 4 + t
            group_copy(n, t, 0, 0).wait_recv()
            s1[at, 2] = (slab(n, t, w) + r1[at, 0].astype(F32)).astype(BF)
            group_copy(n, t, 0, 2).start()

    def line_total(n, t, d):
        at = n * 4 + t
        if t < 2:
            to = m4(x + d)
            own = hp[n, to, z, :, columns(t)]
        else:
            to = m4(z + d)
            own = hp[n, x, to, :, columns(t)]
        return own + r1[at, 1, to].astype(F32) + r1[at, 2, to].astype(F32)

    def group_second(n):
        for t in range(4):
            w = 1 - 2 * (t % 2)
            at = n * 4 + t
            group_copy(n, t, 0, 1).wait_recv()
            group_copy(n, t, 0, 2).wait_recv()
            s2[at, 0] = line_total(n, t, 2).astype(BF)
            group_copy(n, t, 1, 0).start()
            s2[at, 1] = line_total(n, t, -w).astype(BF)
            group_copy(n, t, 1, 1).start()

    def group_second_combine(n):
        for t in range(4):
            w = 1 - 2 * (t % 2)
            at = n * 4 + t
            group_copy(n, t, 1, 0).wait_recv()
            s2[at, 2] = (line_total(n, t, w) + r2[at, 0].astype(F32)).astype(BF)
            group_copy(n, t, 1, 2).start()

    def group_last(n):
        j = m4(y + GROUPS[n])
        rows = pl.ds(pl.multiple_of(j * 32, 32), 32)
        for t in range(4):
            at = n * 4 + t
            group_copy(n, t, 1, 1).wait_recv()
            group_copy(n, t, 1, 2).wait_recv()
            value = line_total(n, t, 0) + r2[at, 1].astype(F32) + r2[at, 2].astype(F32)
            gi[rows, columns(t)] = value.astype(BF)

    h_gather.from_sibling(0)
    group_partial(0)
    advance(x_steps, 2)
    h_gather.near()
    h_gather.other()
    group_combine(0)
    h_gather.from_sibling(1)
    group_partial(1)
    group_second(0)
    h_gather.from_sibling(-1)
    group_partial(2)
    group_combine(1)
    group_second_combine(0)
    h_gather.far()
    h_gather.from_sibling(2)
    group_partial(3)
    group_combine(2)
    group_second(1)
    group_combine(3)
    group_last(0)
    advance(x_steps, 4)
    weight_tile(xx, ga, mg, gg_out, 0, 256, 896)
    group_second(2)
    group_second_combine(1)
    group_second(3)
    weight_tile(xx, ga, mg, gg_out, 1, 256, 896)
    group_second_combine(2)
    group_second_combine(3)
    weight_tile(xx, ga, mg, gg_out, 2, 256, 896)
    group_last(1)
    weight_tile(xx, ga, mg, gg_out, 3, 256, 896)
    group_last(2)
    group_last(3)
    gi_copy = pltpu.make_async_copy(gi, gi_out, lsem.at[0])
    gi_copy.start()
    for i in range(4):
        weight_tile(xx, ua, mu, gu_out, i, 256, 896)
    weight_tile(act, dy, md, gd_out, 2, 256, 1024)
    weight_tile(act, dy, md, gd_out, 3, 128, 1024)

    for copy in outs[-4:]:
        copy.wait()
    gi_copy.wait()
    dy_gather.finish()
    x_gather.finish()
    h_gather.finish()

    def drain(at, carry):
        for kind in range(3):
            remote(s1.at[0, 0], r1.at[0, 0], gs.at[at, 0, kind], gr.at[0, 0, 0], sibling).wait_send()
            remote(s2.at[0, 0], r2.at[0, 0], gs.at[at, 1, kind], gr.at[0, 1, 0], sibling).wait_send()
        return carry

    lax.fori_loop(0, 16, drain, 0)


def per_device(
    inputs, grad_out, gate_pre, up_pre, w_gate, w_up, w_down, mask_gate, mask_up, mask_down
):
    anywhere = pl.BlockSpec(memory_space=pl.ANY)
    scalars = pl.BlockSpec(memory_space=pltpu.SMEM)
    dma = pltpu.SemaphoreType.DMA
    flops = 2 * 2048 * 1024 * 896 * 6
    return pl.pallas_call(
        kernel,
        out_shape=[
            jax.ShapeDtypeStruct((128, 1024), BF),
            jax.ShapeDtypeStruct((1024, 896), BF),
            jax.ShapeDtypeStruct((1024, 896), BF),
            jax.ShapeDtypeStruct((896, 1024), BF),
        ],
        in_specs=[anywhere] * 7 + [scalars] * 3,
        out_specs=[anywhere] * 4,
        scratch_shapes=[
            pltpu.VMEM((16, 128, 1024), BF),
            pltpu.VMEM((16, 128, 1024), BF),
            pltpu.VMEM((16, 128, 896), BF),
            pltpu.VMEM((16, 128, 896), BF),
            pltpu.VMEM((8, 2, 4, 32, 896), BF),
            pltpu.VMEM((16, 128, 896), BF),
            pltpu.VMEM((1024, 896), BF),
            pltpu.VMEM((1024, 896), BF),
            pltpu.VMEM((896, 1024), BF),
            pltpu.VMEM((4, 4, 4, 32, 1024), F32),
            pltpu.VMEM((4, 2, 4, 32, 896), F32),
            pltpu.VMEM((6, 4, 32, 896), BF),
            pltpu.VMEM((6, 4, 32, 896), BF),
            pltpu.VMEM((16, 3, 4, 32, 256), BF),
            pltpu.VMEM((16, 3, 4, 32, 256), BF),
            pltpu.VMEM((16, 3, 32, 256), BF),
            pltpu.VMEM((16, 3, 32, 256), BF),
            pltpu.VMEM((128, 1024), BF),
            pltpu.VMEM((4, 256, 1024), BF),
            dma((9,)),
            dma((4,)),
            dma((2, 60)),
            dma((2, 4, 16)),
            dma((3, 14)),
            dma((3, 2, 8)),
            dma((4,)),
            dma((4,)),
            dma((6,)),
            dma((6,)),
            dma((16, 2, 3)),
            dma((16, 2, 3)),
        ],
        compiler_params=pltpu.CompilerParams(
            collective_id=0, has_side_effects=True, vmem_limit_bytes=62 * 2**20
        ),
        cost_estimate=pl.CostEstimate(flops=flops, bytes_accessed=18 * 2**20, transcendentals=4 * 2048 * 896),
    )(inputs, grad_out, gate_pre, up_pre, w_gate, w_up, w_down, mask_gate, mask_up, mask_down)


def solution(mesh):
    placed = (
        P("col", "row"),
        P("col", "row"),
        P("row", "col"),
        P("row", "col"),
        P("row", "col"),
        P("row", "col"),
        P("col", "row"),
        P("row", "col"),
        P("row", "col"),
        P("col", "row"),
    )
    return jax.shard_map(
        per_device,
        mesh=mesh,
        in_specs=placed,
        out_specs=(P("col", "row"), P("row", "col"), P("row", "col"), P("col", "row")),
        check_vma=False,
    )
```

```python
import jax
import jax.numpy as jnp
from jax import lax
from jax.experimental import pallas as pl
from jax.experimental.pallas import tpu as pltpu
from jax.sharding import PartitionSpec as P

MESH = pl.DeviceIdType.MESH
BF = jnp.bfloat16
F32 = jnp.float32
NT = (((1,), (1,)), ((), ()))
TN = (((0,), (0,)), ((), ()))
RELS = (2, 1, -1, 0)
GROUPS = (0, 1, -1, 2)


def m4(value):
    return lax.rem(value + 8, 4)


def coords():
    row, col = lax.axis_index("row"), lax.axis_index("col")
    return lax.div(row, 2), lax.rem(row, 2), lax.div(col, 4), lax.rem(col, 4)


def device(y, k, x, z):
    return {"row": y * 2 + k, "col": x * 4 + z}


def remote(src, dst, send, recv, to):
    return pltpu.make_async_remote_copy(
        src_ref=src, dst_ref=dst, send_sem=send, recv_sem=recv, device_id=to, device_id_type=MESH
    )


class ColGather:
    def __init__(self, full, send, recv, at, rows):
        self.full, self.send_sem, self.recv_sem = full, send, recv
        self.at, self.rows = at, rows
        self.y, self.k, self.x, self.z = coords()

    def piece(self, q, c):
        return self.full.at[c, pl.ds(pl.multiple_of(q * 32 + self.at, 16), self.rows)]

    def index(self, q, a, b):
        late = lax.div(q, 2)
        return m4(self.x + a * (1 - late) + b * late) * 4 + m4(self.z + a * late + b * (1 - late))

    def send(self, q, a, b, second, d, slot):
        c = self.index(q, a, b)
        late = lax.div(q, 2)
        along_z = late + second - 2 * late * second
        to = device(self.y, self.k, m4(self.x + d * (1 - along_z)), m4(self.z + d * along_z))
        remote(
            self.piece(q, c), self.piece(q, c), self.send_sem.at[q * 15 + slot], self.recv_sem.at[q, c], to
        ).start()

    def recv(self, q, a, b):
        c = self.index(q, a, b)
        remote(
            self.piece(q, c),
            self.piece(q, c),
            self.send_sem.at[0],
            self.recv_sem.at[q, c],
            device(self.y, self.k, m4(self.x + 1), self.z),
        ).wait_recv()

    def each(self, body):
        def step(q, carry):
            body(q, 1 - 2 * lax.rem(q, 2))
            return carry

        lax.fori_loop(0, 4, step, 0)

    def start(self):
        def own(q, w):
            self.send(q, 0, 0, 0, 1, 0)
            self.send(q, 0, 0, 0, -1, 1)

        def own_second(q, w):
            self.send(q, 0, 0, 1, 1, 2)
            self.send(q, 0, 0, 1, -1, 3)

        self.each(own)
        self.each(own_second)

    def step(self, number):
        def first(q, w):
            self.recv(q, -w, 0)
            self.send(q, -w, 0, 0, w, 4)
            self.send(q, -w, 0, 1, 1, 5)
            self.send(q, -w, 0, 1, -1, 6)

        def second(q, w):
            self.recv(q, w, 0)
            self.send(q, w, 0, 1, 1, 7)
            self.send(q, w, 0, 1, -1, 8)

        def own_line(q, w):
            self.recv(q, 0, -w)
            self.send(q, 0, -w, 1, w, 9)

        def far(q, w):
            self.recv(q, 2, 0)
            self.send(q, 2, 0, 1, 1, 10)
            self.send(q, 2, 0, 1, -1, 11)

        def line(q, w):
            a = (-1, 1, 2)[number - 4]
            self.recv(q, a * w, -w)
            self.send(q, a * w, -w, 1, w, 8 + number)

        def last(q, w):
            a = (0, -1, 1, 2)[number - 7]
            self.recv(q, a * w, w)
            self.recv(q, a * w, 2)

        self.each((first, second, own_line, far, line, line, line, last, last, last, last)[number])

    def finish(self):
        def one(i, carry):
            remote(
                self.piece(0, 0),
                self.piece(0, 0),
                self.send_sem.at[i],
                self.recv_sem.at[0, 0],
                device(self.y, self.k, m4(self.x + 1), self.z),
            ).wait_send()
            return carry

        lax.fori_loop(0, 60, one, 0)


class RowGather:
    def __init__(self, view, send, recv):
        self.view, self.send_sem, self.recv_sem = view, send, recv
        self.y, self.k, self.x, self.z = coords()

    def row(self, dy, sibling=False):
        return m4(self.y + dy) * 2 + (1 - self.k if sibling else self.k)

    def sibling(self):
        return device(self.y, 1 - self.k, self.x, self.z)

    def copy(self, p, h, r, slot, to):
        view = self.view(r, p, h)
        return remote(view, view, self.send_sem.at[p * 14 + h * 7 + slot], self.recv_sem.at[p, h, r], to)

    def ring(self, p, h, dy, d, slot):
        to = device(m4(self.y + d), self.k, self.x, self.z)
        self.copy(p, h, self.row(dy), slot, to).start()

    def cross(self, p, h, dy, slot):
        self.copy(p, h, self.row(dy), slot, self.sibling()).start()

    def recv(self, p, h, dy, sibling=False):
        self.copy(p, h, self.row(dy, sibling), 0, self.sibling()).wait_recv()

    def start(self, p):
        self.ring(p, 0, 0, 1, 0)
        self.ring(p, 1, 0, -1, 1)
        self.ring(p, 1, 0, 1, 0)
        self.ring(p, 0, 0, -1, 1)
        self.cross(p, 0, 0, 2)
        self.cross(p, 1, 0, 2)

    def near(self, p):
        for h in (0, 1):
            w = 1 - 2 * h
            self.recv(p, h, -w)
            self.ring(p, h, -w, w, 3)
            self.cross(p, h, -w, 4)

    def other(self, p):
        for h in (0, 1):
            w = 1 - 2 * h
            self.recv(p, h, w)
            self.cross(p, h, w, 5)

    def far(self, p):
        for h in (0, 1):
            self.recv(p, h, 2)
            self.cross(p, h, 2, 6)

    def from_sibling(self, p, dy):
        for h in (0, 1):
            self.recv(p, h, dy, True)

    def finish(self, p):
        for h in (0, 1):
            for slot in range(7):
                self.copy(p, h, 0, slot, self.sibling()).wait_send()


def kernel(
    x_in, dy_in, g_in, u_in, wg_in, wu_in, wd_in, mg, mu, md,
    gi_out, gg_out, gu_out, gd_out,
    dy, xx, ga, ua, hd, act, wg, wu, wd, hp, pa, rb, ys, yr, s1, r1, s2, r2, gi, stage,
    lsem, osem, col_s, col_r, row_s, row_r, sib_s, sib_r, ring_s, ring_r, gs, gr,
):
    y, k, x, z = coords()
    me_col, me_row = x * 4 + z, y * 2 + k
    sibling = device(y, 1 - k, x, z)
    up_y, down_y = device(m4(y + 1), k, x, z), device(m4(y - 1), k, x, z)

    two = pl.ds(2 * me_row, 2)
    local = [
        pltpu.make_async_copy(dy_in, dy.at[me_col], lsem.at[0]),
        pltpu.make_async_copy(g_in, ga.at[two], lsem.at[1]),
        pltpu.make_async_copy(u_in, ua.at[two], lsem.at[2]),
        pltpu.make_async_copy(wd_in, wd, lsem.at[3]),
        pltpu.make_async_copy(x_in, xx.at[me_col], lsem.at[4]),
        pltpu.make_async_copy(wg_in, wg, lsem.at[5]),
        pltpu.make_async_copy(wu_in, wu, lsem.at[6]),
    ]
    for copy in local:
        copy.start()

    barrier = pltpu.get_barrier_semaphore()
    for to in (
        device(y, k, m4(x + 1), z),
        device(y, k, m4(x - 1), z),
        device(y, k, x, m4(z + 1)),
        device(y, k, x, m4(z - 1)),
        device(y, k, m4(x + 2), z),
        device(y, k, x, m4(z + 2)),
        up_y,
        down_y,
        sibling,
    ):
        pl.semaphore_signal(barrier, inc=1, device_id=to, device_id_type=MESH)
    pl.semaphore_wait(barrier, 9)

    dy_gathers = [ColGather(dy, col_s.at[p], col_r.at[p], 16 * p, 16) for p in range(2)]
    x_gather = ColGather(xx, col_s.at[2], col_r.at[2], 0, 32)
    g_gather = RowGather(lambda r, p, h: ga.at[2 * r + h, :, p], row_s.at[0], row_r.at[0])
    u_gather = RowGather(lambda r, p, h: ua.at[2 * r + h, :, p], row_s.at[1], row_r.at[1])
    h_gather = RowGather(lambda r, p, h: hd.at[r, p, h], row_s.at[2], row_r.at[2])

    def apply_mask(w, mask, rows, columns):
        def line(i, carry):
            here = pl.ds(pl.multiple_of(i * 128, 128), 128)
            for j in range(columns):
                keep = mask[i, j].astype(F32)
                block = w[here, j * 128 : (j + 1) * 128].astype(F32)
                w[here, j * 128 : (j + 1) * 128] = (block * keep).astype(BF)
            return carry

        lax.fori_loop(0, rows, line, 0)

    def across(p, slot):
        there, rows = pl.ds(2 * (1 - k), 2), pl.ds(16 * p, 16)
        return remote(
            hp.at[slot, there, :, rows, pl.ds(0, 896)],
            rb.at[slot, :, :, rows],
            sib_s.at[p, slot],
            sib_r.at[p, slot],
            sibling,
        )

    def partial(p, slot):
        j = m4(y + RELS[slot])
        rows = pl.ds(pl.multiple_of(j * 32 + p * 16, 16), 16)
        left = dy[:, rows, :].reshape(256, 1024)
        product = lax.dot_general(left, wd[...], NT, preferred_element_type=F32)
        hp[slot, :, :, p * 16 : p * 16 + 16, 0:896] = product.reshape(4, 4, 16, 896)
        across(p, slot).start()

    def total(p, slot, h, i):
        rows = pl.ds(p * 16, 16)
        return hp[slot, 2 * k + h, i, rows, 0:896] + rb[slot, h, i, rows]

    def ring_copy(p, n):
        to = up_y if n % 2 == 0 else down_y
        return remote(ys.at[p, n], yr.at[p, n], ring_s.at[p, n], ring_r.at[p, n], to)

    def pack(p, n, slot, h, with_recv=None):
        if with_recv is not None:
            ring_copy(p, with_recv).wait_recv()

        def one(i, carry):
            value = total(p, slot, h, i)
            if with_recv is not None:
                value = value + yr[p, with_recv, i].astype(F32)
            ys[p, n, i] = value.astype(BF)
            return carry

        lax.fori_loop(0, 4, one, 0)
        ring_copy(p, n).start()

    def pack_far(p):
        pack(p, 0, 0, 0)
        pack(p, 1, 0, 1)

    def pack_near(p):
        pack(p, 2, 1, 1)
        pack(p, 3, 2, 0)

    def pack_sum(p):
        pack(p, 4, 1, 0, 0)
        pack(p, 5, 2, 1, 1)

    def finish_hidden(p):
        for h, first, second in ((0, 3, 4), (1, 2, 5)):
            ring_copy(p, first).wait_recv()
            ring_copy(p, second).wait_recv()

            def one(i, carry, h=h, first=first, second=second):
                value = total(p, 3, h, i) + yr[p, first, i].astype(F32) + yr[p, second, i].astype(F32)
                hd[me_row, p, h, i] = value.astype(BF)
                return carry

            lax.fori_loop(0, 4, one, 0)
        h_gather.start(p)

    def activation(p):
        def one(c, carry):
            for j in range(4):
                gated = ga[c, j, p].astype(F32)
                act[c, j, p] = (gated * jax.nn.sigmoid(gated) * ua[c, j, p].astype(F32)).astype(BF)
            return carry

        lax.fori_loop(0, 16, one, 0)

    outs = []

    def weight_tile(left, right, mask, out, i, rows, columns):
        slot = len(outs) % 4
        if len(outs) >= 4:
            outs[len(outs) - 4].wait()
        copy = pltpu.make_async_copy(
            stage.at[slot, pl.ds(0, rows), pl.ds(0, columns)], out.at[pl.ds(i * 256, rows)], osem.at[slot]
        )
        if left is act:
            a = left[:, :, :, :, i * 256 : i * 256 + rows].reshape(2048, rows)
        else:
            a = left[:, :, i * 256 : i * 256 + rows].reshape(2048, rows)
        b = right[...].reshape(2048, columns)
        product = lax.dot_general(a, b, TN, preferred_element_type=F32)
        for p in range(rows // 128):
            for q in range(columns // 128):
                keep = mask[i * 2 + p, q].astype(F32)
                block = product[p * 128 : (p + 1) * 128, q * 128 : (q + 1) * 128]
                stage[slot, p * 128 : (p + 1) * 128, q * 128 : (q + 1) * 128] = (block * keep).astype(BF)
        copy.start()
        outs.append(copy)

    def down_tile(i):
        weight_tile(act, dy, md, gd_out, i, 256 if i < 3 else 128, 1024)

    def gate_tile(i):
        weight_tile(xx, ga, mg, gg_out, i, 256, 896)

    def up_tile(i):
        weight_tile(xx, ua, mu, gu_out, i, 256, 896)

    offsets = (2, 1, -1)

    def group_copy(p, n, t, stage_at, i):
        d = offsets[i]
        if t == stage_at:
            to = device(y, k, x, m4(z + d))
        else:
            to = device(y, k, m4(x + d), z)
        at = p * 8 + n * 2 + t
        src, dst = (s1, r1) if stage_at == 0 else (s2, r2)
        return remote(src.at[at, i], dst.at[at, i], gs.at[at, stage_at, i], gr.at[at, stage_at, i], to)

    def columns(t):
        return pl.ds(t * 512, 512)

    def partials(p):
        return pa if p == 0 else hp

    def group_partial(p, n):
        j = m4(y + GROUPS[n])

        def one(c, carry):
            gated = ga[c, j, p].astype(F32)
            upper = ua[c, j, p].astype(F32)
            hidden = hd[2 * j + lax.div(c, 8), p, lax.rem(lax.div(c, 4), 2), lax.rem(c, 4)].astype(F32)
            sigma = jax.nn.sigmoid(gated)
            ga[c, j, p] = (hidden * upper * sigma * (1.0 + gated * (1.0 - sigma))).astype(BF)
            ua[c, j, p] = (hidden * gated * sigma).astype(BF)
            return carry

        lax.fori_loop(0, 16, one, 0)
        product = lax.dot_general(ga[:, j, p].reshape(256, 896), wg[...], NT, preferred_element_type=F32)
        product = product + lax.dot_general(
            ua[:, j, p].reshape(256, 896), wu[...], NT, preferred_element_type=F32
        )
        partials(p)[n, :, :, 0:16, :] = product.reshape(4, 4, 16, 1024)
        for i, d in enumerate(offsets):
            s1[p * 8 + n * 2, i] = partials(p)[n, :, m4(z + d), 0:16, columns(0)].astype(BF)
            group_copy(p, n, 0, 0, i).start()
            s1[p * 8 + n * 2 + 1, i] = partials(p)[n, m4(x + d), :, 0:16, columns(1)].astype(BF)
            group_copy(p, n, 1, 0, i).start()

    def line_total(p, n, t, d):
        at = p * 8 + n * 2 + t
        if t == 0:
            to = m4(x + d)
            own = partials(p)[n, to, z, 0:16, columns(t)]
        else:
            to = m4(z + d)
            own = partials(p)[n, x, to, 0:16, columns(t)]
        for i in range(3):
            own = own + r1[at, i, to].astype(F32)
        return own

    def group_second(p, n):
        for t in range(2):
            for i in range(3):
                group_copy(p, n, t, 0, i).wait_recv()
        for i, d in enumerate(offsets):
            for t in range(2):
                s2[p * 8 + n * 2 + t, i] = line_total(p, n, t, d).astype(BF)
                group_copy(p, n, t, 1, i).start()

    def group_last(p, n):
        j = m4(y + GROUPS[n])
        rows = pl.ds(pl.multiple_of(j * 32 + p * 16, 16), 16)
        for t in range(2):
            value = line_total(p, n, t, 0)
            for i in range(3):
                group_copy(p, n, t, 1, i).wait_recv()
                value = value + r2[p * 8 + n * 2 + t, i].astype(F32)
            gi[rows, columns(t)] = value.astype(BF)

    local[0].wait()
    dy_gathers[0].start()
    local[1].wait()
    g_gather.start(0)
    local[2].wait()
    u_gather.start(0)
    local[3].wait()
    apply_mask(wd, md, 7, 8)
    local[5].wait()
    apply_mask(wg, mg, 8, 7)
    local[6].wait()
    apply_mask(wu, mu, 8, 7)
    dy_gathers[0].step(0)
    dy_gathers[1].start()
    dy_gathers[0].step(1)
    dy_gathers[0].step(2)
    g_gather.near(0)
    g_gather.other(0)
    dy_gathers[0].step(3)
    dy_gathers[0].step(4)
    dy_gathers[1].step(0)
    dy_gathers[1].step(1)
    u_gather.near(0)
    g_gather.start(1)
    u_gather.start(1)
    dy_gathers[1].step(2)
    dy_gathers[0].step(5)
    u_gather.other(0)
    dy_gathers[0].step(6)
    dy_gathers[0].step(7)
    g_gather.far(0)
    dy_gathers[0].step(8)
    dy_gathers[1].step(3)
    dy_gathers[1].step(4)
    dy_gathers[1].step(5)
    g_gather.near(1)
    dy_gathers[0].step(9)
    dy_gathers[0].step(10)
    partial(0, 0)
    partial(0, 1)
    dy_gathers[1].step(6)
    dy_gathers[1].step(7)
    local[4].wait()
    x_gather.start()
    dy_gathers[1].step(8)
    partial(0, 2)
    across(0, 0).wait_recv()
    pack_far(0)
    dy_gathers[1].step(9)
    partial(0, 3)
    u_gather.near(1)
    u_gather.far(0)
    g_gather.other(1)
    across(0, 1).wait_recv()
    across(0, 2).wait_recv()
    pack_near(0)
    dy_gathers[1].step(10)
    partial(1, 0)
    partial(1, 1)
    u_gather.other(1)
    for offset in (0, 1, -1, 2):
        g_gather.from_sibling(0, offset)
        u_gather.from_sibling(0, offset)
    activation(0)
    g_gather.finish(0)
    u_gather.finish(0)
    across(1, 0).wait_recv()
    pack_far(1)
    x_gather.step(0)
    x_gather.step(1)
    g_gather.far(1)
    partial(1, 2)
    partial(1, 3)
    x_gather.step(2)
    pack_sum(0)
    across(1, 1).wait_recv()
    across(1, 2).wait_recv()
    pack_near(1)
    u_gather.far(1)
    for offset in (0, 1, -1, 2):
        g_gather.from_sibling(1, offset)
        u_gather.from_sibling(1, offset)
    x_gather.step(3)
    x_gather.step(4)
    activation(1)
    g_gather.finish(1)
    u_gather.finish(1)
    down_tile(1)
    x_gather.step(5)
    down_tile(0)
    pack_sum(1)
    down_tile(3)
    across(0, 3).wait_recv()
    finish_hidden(0)
    down_tile(2)
    h_gather.from_sibling(0, 0)
    group_partial(0, 0)
    x_gather.step(6)
    x_gather.step(7)
    x_gather.step(8)
    x_gather.step(9)
    across(1, 3).wait_recv()
    finish_hidden(1)
    for p in range(2):
        for slot in range(4):
            across(p, slot).wait_send()
    h_gather.from_sibling(1, 0)
    group_partial(1, 0)
    h_gather.near(0)
    group_second(0, 0)
    h_gather.other(0)
    x_gather.step(10)
    h_gather.from_sibling(0, 1)
    group_partial(0, 1)
    h_gather.near(1)
    h_gather.from_sibling(0, -1)
    group_partial(0, 2)
    h_gather.other(1)
    group_second(1, 0)
    group_last(0, 0)
    h_gather.from_sibling(1, 1)
    group_partial(1, 1)
    h_gather.far(0)
    h_gather.from_sibling(1, -1)
    group_partial(1, 2)
    h_gather.far(1)
    h_gather.from_sibling(0, 2)
    group_partial(0, 3)
    h_gather.from_sibling(1, 2)
    group_partial(1, 3)
    group_second(1, 1)
    group_second(0, 2)
    group_second(0, 1)
    gate_tile(3)
    group_second(1, 2)
    group_last(1, 0)
    up_tile(3)
    up_tile(0)
    group_second(0, 3)
    up_tile(1)
    up_tile(2)
    group_second(1, 3)
    group_last(1, 1)
    gate_tile(0)
    group_last(0, 2)
    group_last(0, 1)
    group_last(1, 2)
    gate_tile(1)
    group_last(0, 3)
    gate_tile(2)
    group_last(1, 3)
    for p in range(2):
        for n in range(6):
            ring_copy(p, n).wait_send()

    gi_copy = pltpu.make_async_copy(gi, gi_out, lsem.at[0])
    gi_copy.start()
    for copy in outs[-4:]:
        copy.wait()
    gi_copy.wait()
    dy_gathers[0].finish()
    dy_gathers[1].finish()
    x_gather.finish()
    h_gather.finish(0)
    h_gather.finish(1)

    def drain(at, carry):
        for kind in range(3):
            remote(s1.at[0, 0], r1.at[0, 0], gs.at[at, 0, kind], gr.at[0, 0, 0], sibling).wait_send()
            remote(s2.at[0, 0], r2.at[0, 0], gs.at[at, 1, kind], gr.at[0, 1, 0], sibling).wait_send()
        return carry

    lax.fori_loop(0, 16, drain, 0)


def hand_over(*refs):
    sources, targets, held, come, gone = refs[:4], refs[4:8], refs[8:12], refs[12], refs[13]
    parts = []
    for source, target, hold in zip(sources, targets, held, strict=True):
        rows = source.shape[0] // 4
        for part in range(4):
            here, n = pl.ds(part * rows, rows), len(parts)
            parts.append(
                (
                    pltpu.make_async_copy(source.at[here], hold.at[here], come.at[n]),
                    pltpu.make_async_copy(hold.at[here], target.at[here], gone.at[n]),
                )
            )
    for first, _ in parts:
        first.start()
    for first, second in parts:
        first.wait()
        second.start()
    for _, second in parts:
        second.wait()


def per_device(
    inputs, grad_out, gate_pre, up_pre, w_gate, w_up, w_down, mask_gate, mask_up, mask_down
):
    anywhere = pl.BlockSpec(memory_space=pl.ANY)
    scalars = pl.BlockSpec(memory_space=pltpu.SMEM)
    dma = pltpu.SemaphoreType.DMA
    flops = 2 * 2048 * 1024 * 896 * 6
    shapes = [
        jax.ShapeDtypeStruct((128, 1024), BF),
        jax.ShapeDtypeStruct((1024, 896), BF),
        jax.ShapeDtypeStruct((1024, 896), BF),
        jax.ShapeDtypeStruct((896, 1024), BF),
    ]
    gate_parts = gate_pre.reshape(2, 4, 2, 16, 896)
    up_parts = up_pre.reshape(2, 4, 2, 16, 896)
    results = pl.pallas_call(
        kernel,
        out_shape=shapes,
        in_specs=[anywhere] * 7 + [scalars] * 3,
        out_specs=[anywhere] * 4,
        scratch_shapes=[
            pltpu.VMEM((16, 128, 1024), BF),
            pltpu.VMEM((16, 128, 1024), BF),
            pltpu.VMEM((16, 4, 2, 16, 896), BF),
            pltpu.VMEM((16, 4, 2, 16, 896), BF),
            pltpu.VMEM((8, 2, 2, 4, 16, 896), BF),
            pltpu.VMEM((16, 4, 2, 16, 896), BF),
            pltpu.VMEM((1024, 896), BF),
            pltpu.VMEM((1024, 896), BF),
            pltpu.VMEM((896, 1024), BF),
            pltpu.VMEM((4, 4, 4, 32, 1024), F32),
            pltpu.VMEM((4, 4, 4, 16, 1024), F32),
            pltpu.VMEM((4, 2, 4, 32, 896), F32),
            pltpu.VMEM((2, 6, 4, 16, 896), BF),
            pltpu.VMEM((2, 6, 4, 16, 896), BF),
            pltpu.VMEM((16, 3, 4, 16, 512), BF),
            pltpu.VMEM((16, 3, 4, 16, 512), BF),
            pltpu.VMEM((16, 3, 16, 512), BF),
            pltpu.VMEM((16, 3, 16, 512), BF),
            pltpu.VMEM((128, 1024), BF),
            pltpu.VMEM((4, 256, 1024), BF),
            dma((7,)),
            dma((4,)),
            dma((3, 60)),
            dma((3, 4, 16)),
            dma((3, 28)),
            dma((3, 2, 2, 8)),
            dma((2, 4)),
            dma((2, 4)),
            dma((2, 6)),
            dma((2, 6)),
            dma((16, 2, 3)),
            dma((16, 2, 3)),
        ],
        compiler_params=pltpu.CompilerParams(
            collective_id=0, has_side_effects=True, vmem_limit_bytes=62 * 2**20
        ),
        cost_estimate=pl.CostEstimate(flops=flops, bytes_accessed=18 * 2**20, transcendentals=4 * 2048 * 896),
    )(inputs, grad_out, gate_parts, up_parts, w_gate, w_up, w_down, mask_gate, mask_up, mask_down)
    return pl.pallas_call(
        hand_over,
        out_shape=shapes,
        in_specs=[anywhere] * 4,
        out_specs=[anywhere] * 4,
        scratch_shapes=[pltpu.VMEM(shape.shape, BF) for shape in shapes] + [dma((16,)), dma((16,))],
        compiler_params=pltpu.CompilerParams(vmem_limit_bytes=62 * 2**20),
        cost_estimate=pl.CostEstimate(flops=0, bytes_accessed=12 * 2**20, transcendentals=0),
    )(*results)


def solution(mesh):
    placed = (
        P("col", "row"),
        P("col", "row"),
        P("row", "col"),
        P("row", "col"),
        P("row", "col"),
        P("row", "col"),
        P("col", "row"),
        P("row", "col"),
        P("row", "col"),
        P("col", "row"),
    )
    return jax.shard_map(
        per_device,
        mesh=mesh,
        in_specs=placed,
        out_specs=(P("col", "row"), P("row", "col"), P("row", "col"), P("col", "row")),
        check_vma=False,
    )
```

```python
import jax
import jax.numpy as jnp
from jax import lax
from jax.experimental import pallas as pl
from jax.experimental.pallas import tpu as pltpu
from jax.sharding import PartitionSpec as P

MESH = pl.DeviceIdType.MESH
BF = jnp.bfloat16
F32 = jnp.float32
NT = (((1,), (1,)), ((), ()))
TN = (((0,), (0,)), ((), ()))
RELS = (2, 1, -1, 0)
GROUPS = (0, 1, -1, 2)


def m4(value):
    return lax.rem(value + 8, 4)


def coords():
    row, col = lax.axis_index("row"), lax.axis_index("col")
    return lax.div(row, 2), lax.rem(row, 2), lax.div(col, 4), lax.rem(col, 4)


def device(y, k, x, z):
    return {"row": y * 2 + k, "col": x * 4 + z}


def remote(src, dst, send, recv, to):
    return pltpu.make_async_remote_copy(
        src_ref=src, dst_ref=dst, send_sem=send, recv_sem=recv, device_id=to, device_id_type=MESH
    )


class ColGather:
    def __init__(self, full, send, recv, at, rows):
        self.full, self.send_sem, self.recv_sem = full, send, recv
        self.at, self.rows = at, rows
        self.y, self.k, self.x, self.z = coords()

    def piece(self, q, c):
        return self.full.at[c, pl.ds(pl.multiple_of(q * 32 + self.at, 16), self.rows)]

    def index(self, q, a, b):
        late = lax.div(q, 2)
        return m4(self.x + a * (1 - late) + b * late) * 4 + m4(self.z + a * late + b * (1 - late))

    def send(self, q, a, b, second, d, slot):
        c = self.index(q, a, b)
        late = lax.div(q, 2)
        along_z = late + second - 2 * late * second
        to = device(self.y, self.k, m4(self.x + d * (1 - along_z)), m4(self.z + d * along_z))
        remote(
            self.piece(q, c), self.piece(q, c), self.send_sem.at[q * 15 + slot], self.recv_sem.at[q, c], to
        ).start()

    def recv(self, q, a, b):
        c = self.index(q, a, b)
        remote(
            self.piece(q, c),
            self.piece(q, c),
            self.send_sem.at[0],
            self.recv_sem.at[q, c],
            device(self.y, self.k, m4(self.x + 1), self.z),
        ).wait_recv()

    def each(self, body):
        def step(q, carry):
            body(q, 1 - 2 * lax.rem(q, 2))
            return carry

        lax.fori_loop(0, 4, step, 0)

    def start(self, second):
        def own(q, w):
            self.send(q, 0, 0, 0, 1, 0)
            self.send(q, 0, 0, 0, -1, 1)

        def own_second(q, w):
            self.send(q, 0, 0, 1, 1, 2)
            self.send(q, 0, 0, 1, -1, 3)

        self.each(own_second if second else own)

    def step(self, number):
        def first(q, w):
            self.recv(q, -w, 0)
            self.send(q, -w, 0, 0, w, 4)
            self.send(q, -w, 0, 1, 1, 5)
            self.send(q, -w, 0, 1, -1, 6)

        def second(q, w):
            self.recv(q, w, 0)
            self.send(q, w, 0, 1, 1, 7)
            self.send(q, w, 0, 1, -1, 8)

        def own_line(q, w):
            self.recv(q, 0, -w)
            self.send(q, 0, -w, 1, w, 9)

        def far(q, w):
            self.recv(q, 2, 0)
            self.send(q, 2, 0, 1, 1, 10)
            self.send(q, 2, 0, 1, -1, 11)

        def line(q, w):
            a = (-1, 1, 2)[number - 4]
            self.recv(q, a * w, -w)
            self.send(q, a * w, -w, 1, w, 8 + number)

        def last(q, w):
            a = (0, -1, 1, 2)[number - 7]
            self.recv(q, a * w, w)
            self.recv(q, a * w, 2)

        self.each((first, second, own_line, far, line, line, line, last, last, last, last)[number])

    def finish(self):
        def one(i, carry):
            remote(
                self.piece(0, 0),
                self.piece(0, 0),
                self.send_sem.at[i],
                self.recv_sem.at[0, 0],
                device(self.y, self.k, m4(self.x + 1), self.z),
            ).wait_send()
            return carry

        lax.fori_loop(0, 60, one, 0)


class RowGather:
    def __init__(self, view, send, recv):
        self.view, self.send_sem, self.recv_sem = view, send, recv
        self.y, self.k, self.x, self.z = coords()

    def row(self, dy, sibling=False):
        return m4(self.y + dy) * 2 + (1 - self.k if sibling else self.k)

    def sibling(self):
        return device(self.y, 1 - self.k, self.x, self.z)

    def copy(self, p, h, r, slot, to):
        view = self.view(r, p, h)
        return remote(view, view, self.send_sem.at[p * 14 + h * 7 + slot], self.recv_sem.at[p, h, r], to)

    def ring(self, p, h, dy, d, slot):
        to = device(m4(self.y + d), self.k, self.x, self.z)
        self.copy(p, h, self.row(dy), slot, to).start()

    def cross(self, p, h, dy, slot):
        self.copy(p, h, self.row(dy), slot, self.sibling()).start()

    def recv(self, p, h, dy, sibling=False):
        self.copy(p, h, self.row(dy, sibling), 0, self.sibling()).wait_recv()

    def start(self, p, second):
        self.ring(p, second, 0, 1, 0)
        self.ring(p, 1 - second, 0, -1, 1)
        self.cross(p, second, 0, 2)

    def near(self, p):
        for h in (0, 1):
            w = 1 - 2 * h
            self.recv(p, h, -w)
            self.ring(p, h, -w, w, 3)
            self.cross(p, h, -w, 4)

    def other(self, p):
        for h in (0, 1):
            w = 1 - 2 * h
            self.recv(p, h, w)
            self.cross(p, h, w, 5)

    def far(self, p):
        for h in (0, 1):
            self.recv(p, h, 2)
            self.cross(p, h, 2, 6)

    def from_sibling(self, p, dy):
        for h in (0, 1):
            self.recv(p, h, dy, True)

    def finish(self, p):
        for h in (0, 1):
            for slot in range(7):
                self.copy(p, h, 0, slot, self.sibling()).wait_send()


def kernel(
    x_in, dy_in, g_in, u_in, wg_in, wu_in, wd_in, mg, mu, md,
    gi, gw, gd,
    dy, xx, gu, hd, act, hp, pa, rb, ys, yr, s1, r1, s2, r2,
    lsem, col_s, col_r, row_s, row_r, sib_s, sib_r, ring_s, ring_r, gs, gr,
):
    y, k, x, z = coords()
    me_col, me_row = x * 4 + z, y * 2 + k
    sibling = device(y, 1 - k, x, z)
    up_y, down_y = device(m4(y + 1), k, x, z), device(m4(y - 1), k, x, z)

    two, left_half, right_half = pl.ds(2 * me_row, 2), pl.ds(0, 896), pl.ds(896, 896)
    local = [
        pltpu.make_async_copy(dy_in, dy.at[me_col], lsem.at[0]),
        pltpu.make_async_copy(g_in, gu.at[two, :, :, :, left_half], lsem.at[1]),
        pltpu.make_async_copy(u_in, gu.at[two, :, :, :, right_half], lsem.at[2]),
        pltpu.make_async_copy(wd_in, gd, lsem.at[3]),
        pltpu.make_async_copy(x_in, xx.at[me_col], lsem.at[4]),
        pltpu.make_async_copy(wg_in, gw.at[:, left_half], lsem.at[5]),
        pltpu.make_async_copy(wu_in, gw.at[:, right_half], lsem.at[6]),
    ]
    for copy in local:
        copy.start()

    barrier = pltpu.get_barrier_semaphore()
    for to in (
        device(y, k, m4(x + 1), z),
        device(y, k, m4(x - 1), z),
        device(y, k, x, m4(z + 1)),
        device(y, k, x, m4(z - 1)),
        device(y, k, m4(x + 2), z),
        device(y, k, x, m4(z + 2)),
        up_y,
        down_y,
        sibling,
    ):
        pl.semaphore_signal(barrier, inc=1, device_id=to, device_id_type=MESH)
    pl.semaphore_wait(barrier, 9)

    dy_gathers = [ColGather(dy, col_s.at[p], col_r.at[p], 16 * p, 16) for p in range(2)]
    x_gather = ColGather(xx, col_s.at[2], col_r.at[2], 0, 32)
    g_gather = RowGather(lambda r, p, h: gu.at[2 * r + h, :, p], row_s.at[0], row_r.at[0])
    h_gather = RowGather(lambda r, p, h: hd.at[r, p, h], row_s.at[1], row_r.at[1])

    def apply_mask(w, mask, rows, columns, first=0):
        def line(i, carry):
            here = pl.ds(pl.multiple_of(i * 128, 128), 128)
            for j in range(columns):
                keep = mask[i, j].astype(F32)
                block = w[here, first + j * 128 : first + (j + 1) * 128].astype(F32)
                w[here, first + j * 128 : first + (j + 1) * 128] = (block * keep).astype(BF)
            return carry

        lax.fori_loop(0, rows, line, 0)

    def across(p, slot):
        there, rows = pl.ds(2 * (1 - k), 2), pl.ds(16 * p, 16)
        return remote(
            hp.at[slot, there, :, rows, pl.ds(0, 896)],
            rb.at[slot, :, :, rows],
            sib_s.at[p, slot],
            sib_r.at[p, slot],
            sibling,
        )

    def partial(p, slot):
        j = m4(y + RELS[slot])
        rows = pl.ds(pl.multiple_of(j * 32 + p * 16, 16), 16)
        left = dy[:, rows, :].reshape(256, 1024)
        product = lax.dot_general(left, gd[...], NT, preferred_element_type=F32)
        hp[slot, :, :, p * 16 : p * 16 + 16, 0:896] = product.reshape(4, 4, 16, 896)
        across(p, slot).start()

    def total(p, slot, h, i):
        rows = pl.ds(p * 16, 16)
        return hp[slot, 2 * k + h, i, rows, 0:896] + rb[slot, h, i, rows]

    def ring_copy(p, n):
        to = up_y if n % 2 == 0 else down_y
        return remote(ys.at[p, n], yr.at[p, n], ring_s.at[p, n], ring_r.at[p, n], to)

    def pack(p, n, slot, h, with_recv=None):
        if with_recv is not None:
            ring_copy(p, with_recv).wait_recv()

        def one(i, carry):
            value = total(p, slot, h, i)
            if with_recv is not None:
                value = value + yr[p, with_recv, i].astype(F32)
            ys[p, n, i] = value.astype(BF)
            return carry

        lax.fori_loop(0, 4, one, 0)
        ring_copy(p, n).start()

    def pack_far(p):
        pack(p, 0, 0, 0)
        pack(p, 1, 0, 1)

    def pack_near(p):
        pack(p, 2, 1, 1)
        pack(p, 3, 2, 0)

    def pack_sum(p):
        pack(p, 4, 1, 0, 0)
        pack(p, 5, 2, 1, 1)

    def finish_hidden(p):
        for h, first, second in ((0, 3, 4), (1, 2, 5)):
            ring_copy(p, first).wait_recv()
            ring_copy(p, second).wait_recv()

            def one(i, carry, h=h, first=first, second=second):
                value = total(p, 3, h, i) + yr[p, first, i].astype(F32) + yr[p, second, i].astype(F32)
                hd[me_row, p, h, i] = value.astype(BF)
                return carry

            lax.fori_loop(0, 4, one, 0)
        h_gather.start(p, 0)
        h_gather.start(p, 1)

    def activation(p):
        def one(c, carry):
            for j in range(4):
                gated = gu[c, j, p, :, 0:896].astype(F32)
                upper = gu[c, j, p, :, 896:1792].astype(F32)
                act[c, j, p] = (gated * jax.nn.sigmoid(gated) * upper).astype(BF)
            return carry

        lax.fori_loop(0, 16, one, 0)

    def keep_blocks(product, mask, out, i, rows, columns, first=0):
        for p in range(rows // 128):
            for q in range(columns // 128):
                keep = mask[i * 2 + p, q].astype(F32)
                at = first + q * 128
                block = product[p * 128 : (p + 1) * 128, at : at + 128]
                out[i * 256 + p * 128 : i * 256 + (p + 1) * 128, at : at + 128] = (block * keep).astype(BF)

    def down_tile(i):
        rows = 256 if i < 3 else 128
        a = act[:, :, :, :, i * 256 : i * 256 + rows].reshape(2048, rows)
        b = dy[...].reshape(2048, 1024)
        product = lax.dot_general(a, b, TN, preferred_element_type=F32)
        keep_blocks(product, md, gd, i, rows, 1024)

    def pair_tile(i):
        a = xx[:, :, i * 256 : (i + 1) * 256].reshape(2048, 256)
        b = gu[...].reshape(2048, 1792)
        product = lax.dot_general(a, b, TN, preferred_element_type=F32)
        keep_blocks(product, mg, gw, i, 256, 896)
        keep_blocks(product, mu, gw, i, 256, 896, 896)

    offsets = (2, 1, -1)

    def group_copy(p, n, t, stage_at, i):
        d = offsets[i]
        if t == stage_at:
            to = device(y, k, x, m4(z + d))
        else:
            to = device(y, k, m4(x + d), z)
        at = p * 8 + n * 2 + t
        src, dst = (s1, r1) if stage_at == 0 else (s2, r2)
        return remote(src.at[at, i], dst.at[at, i], gs.at[at, stage_at, i], gr.at[at, stage_at, i], to)

    def columns(t):
        return pl.ds(t * 512, 512)

    def partials(p):
        return pa if p == 0 else hp

    def group_partial(p, n):
        j = m4(y + GROUPS[n])

        def one(c, carry):
            gated = gu[c, j, p, :, 0:896].astype(F32)
            upper = gu[c, j, p, :, 896:1792].astype(F32)
            hidden = hd[2 * j + lax.div(c, 8), p, lax.rem(lax.div(c, 4), 2), lax.rem(c, 4)].astype(F32)
            sigma = jax.nn.sigmoid(gated)
            gu[c, j, p, :, 0:896] = (hidden * upper * sigma * (1.0 + gated * (1.0 - sigma))).astype(BF)
            gu[c, j, p, :, 896:1792] = (hidden * gated * sigma).astype(BF)
            return carry

        lax.fori_loop(0, 16, one, 0)
        product = lax.dot_general(gu[:, j, p].reshape(256, 1792), gw[...], NT, preferred_element_type=F32)
        partials(p)[n, :, :, 0:16, :] = product.reshape(4, 4, 16, 1024)
        for i, d in enumerate(offsets):
            s1[p * 8 + n * 2, i] = partials(p)[n, :, m4(z + d), 0:16, columns(0)].astype(BF)
            group_copy(p, n, 0, 0, i).start()
            s1[p * 8 + n * 2 + 1, i] = partials(p)[n, m4(x + d), :, 0:16, columns(1)].astype(BF)
            group_copy(p, n, 1, 0, i).start()

    def line_total(p, n, t, d):
        at = p * 8 + n * 2 + t
        if t == 0:
            to = m4(x + d)
            own = partials(p)[n, to, z, 0:16, columns(t)]
        else:
            to = m4(z + d)
            own = partials(p)[n, x, to, 0:16, columns(t)]
        for i in range(3):
            own = own + r1[at, i, to].astype(F32)
        return own

    def group_second(p, n):
        for t in range(2):
            for i in range(3):
                group_copy(p, n, t, 0, i).wait_recv()
        for i, d in enumerate(offsets):
            for t in range(2):
                s2[p * 8 + n * 2 + t, i] = line_total(p, n, t, d).astype(BF)
                group_copy(p, n, t, 1, i).start()

    def group_last(p, n):
        j = m4(y + GROUPS[n])
        rows = pl.ds(pl.multiple_of(j * 32 + p * 16, 16), 16)
        for t in range(2):
            value = line_total(p, n, t, 0)
            for i in range(3):
                group_copy(p, n, t, 1, i).wait_recv()
                value = value + r2[p * 8 + n * 2 + t, i].astype(F32)
            gi[rows, columns(t)] = value.astype(BF)

    local[0].wait()
    dy_gathers[0].start(0)
    dy_gathers[0].start(1)
    local[1].wait()
    local[2].wait()
    g_gather.start(0, 0)
    g_gather.start(0, 1)
    g_gather.start(1, 0)
    g_gather.start(1, 1)
    dy_gathers[0].step(0)
    dy_gathers[0].step(1)
    dy_gathers[1].start(0)
    dy_gathers[1].start(1)
    local[4].wait()
    x_gather.start(0)
    dy_gathers[0].step(2)
    g_gather.near(0)
    dy_gathers[0].step(3)
    dy_gathers[0].step(4)
    dy_gathers[0].step(5)
    local[3].wait()
    apply_mask(gd, md, 7, 8)
    local[5].wait()
    apply_mask(gw, mg, 8, 7)
    local[6].wait()
    apply_mask(gw, mu, 8, 7, 896)
    dy_gathers[1].step(0)
    dy_gathers[1].step(1)
    g_gather.other(0)
    dy_gathers[1].step(2)
    g_gather.near(1)
    dy_gathers[0].step(6)
    dy_gathers[0].step(7)
    dy_gathers[0].step(8)
    dy_gathers[0].step(9)
    dy_gathers[1].step(3)
    x_gather.start(1)
    dy_gathers[1].step(4)
    g_gather.other(1)
    dy_gathers[1].step(5)
    dy_gathers[0].step(10)
    partial(0, 0)
    partial(0, 1)
    dy_gathers[1].step(6)
    dy_gathers[1].step(7)
    partial(0, 2)
    across(0, 0).wait_recv()
    pack_far(0)
    partial(0, 3)
    g_gather.far(0)
    x_gather.step(0)
    x_gather.step(1)
    across(0, 1).wait_recv()
    across(0, 2).wait_recv()
    pack_near(0)
    x_gather.step(2)
    dy_gathers[1].step(8)
    dy_gathers[1].step(9)
    for offset in (0, 1, -1, 2):
        g_gather.from_sibling(0, offset)
    activation(0)
    g_gather.finish(0)
    dy_gathers[1].step(10)
    partial(1, 0)
    partial(1, 1)
    partial(1, 2)
    partial(1, 3)
    across(1, 0).wait_recv()
    pack_far(1)
    g_gather.far(1)
    pack_sum(0)
    x_gather.step(3)
    x_gather.step(4)
    across(1, 1).wait_recv()
    across(1, 2).wait_recv()
    pack_near(1)
    for offset in (0, 1, -1, 2):
        g_gather.from_sibling(1, offset)
    activation(1)
    g_gather.finish(1)
    down_tile(2)
    x_gather.step(5)
    down_tile(0)
    pack_sum(1)
    down_tile(1)
    x_gather.step(6)
    across(0, 3).wait_recv()
    finish_hidden(0)
    x_gather.step(7)
    down_tile(3)
    x_gather.step(8)
    h_gather.from_sibling(0, 0)
    group_partial(0, 0)
    x_gather.step(9)
    x_gather.step(10)
    across(1, 3).wait_recv()
    finish_hidden(1)
    for p in range(2):
        for slot in range(4):
            across(p, slot).wait_send()
    h_gather.from_sibling(1, 0)
    group_partial(1, 0)
    h_gather.near(0)
    group_second(0, 0)
    h_gather.other(0)
    h_gather.from_sibling(0, 1)
    group_partial(0, 1)
    h_gather.near(1)
    h_gather.from_sibling(0, -1)
    group_partial(0, 2)
    h_gather.other(1)
    group_last(0, 0)
    group_second(1, 0)
    h_gather.from_sibling(1, 1)
    group_partial(1, 1)
    h_gather.far(0)
    group_second(0, 1)
    h_gather.from_sibling(1, -1)
    group_partial(1, 2)
    h_gather.far(1)
    h_gather.from_sibling(0, 2)
    group_partial(0, 3)
    h_gather.from_sibling(1, 2)
    group_partial(1, 3)
    group_second(1, 1)
    pair_tile(0)
    group_second(1, 2)
    pair_tile(2)
    group_second(0, 3)
    group_second(0, 2)
    pair_tile(1)
    group_second(1, 3)
    group_last(1, 1)
    group_last(0, 1)
    group_last(1, 0)
    pair_tile(3)
    group_last(1, 2)
    group_last(0, 2)
    group_last(0, 3)
    group_last(1, 3)
    for p in range(2):
        for n in range(6):
            ring_copy(p, n).wait_send()

    dy_gathers[0].finish()
    dy_gathers[1].finish()
    x_gather.finish()
    h_gather.finish(0)
    h_gather.finish(1)

    def drain(at, carry):
        for kind in range(3):
            remote(s1.at[0, 0], r1.at[0, 0], gs.at[at, 0, kind], gr.at[0, 0, 0], sibling).wait_send()
            remote(s2.at[0, 0], r2.at[0, 0], gs.at[at, 1, kind], gr.at[0, 1, 0], sibling).wait_send()
        return carry

    lax.fori_loop(0, 16, drain, 0)


def hand_over(gi, gw, gd, gi_out, gg_out, gu_out, gd_out, sems):
    copies = [
        (gw.at[:, pl.ds(0, 896)], gg_out),
        (gw.at[:, pl.ds(896, 896)], gu_out),
        (gd, gd_out),
        (gi, gi_out),
    ]
    copies = [pltpu.make_async_copy(src, dst, sems.at[n]) for n, (src, dst) in enumerate(copies)]
    for copy in copies:
        copy.start()
    for copy in copies:
        copy.wait()


def per_device(
    inputs, grad_out, gate_pre, up_pre, w_gate, w_up, w_down, mask_gate, mask_up, mask_down
):
    anywhere = pl.BlockSpec(memory_space=pl.ANY)
    scalars = pl.BlockSpec(memory_space=pltpu.SMEM)
    vmem = pl.BlockSpec(memory_space=pltpu.VMEM)
    held = [pltpu.VMEM((128, 1024), BF), pltpu.VMEM((1024, 1792), BF), pltpu.VMEM((896, 1024), BF)]
    dma = pltpu.SemaphoreType.DMA
    flops = 2 * 2048 * 1024 * 896 * 6
    shapes = [
        jax.ShapeDtypeStruct((128, 1024), BF),
        jax.ShapeDtypeStruct((1024, 896), BF),
        jax.ShapeDtypeStruct((1024, 896), BF),
        jax.ShapeDtypeStruct((896, 1024), BF),
    ]
    gate_parts = gate_pre.reshape(2, 4, 2, 16, 896)
    up_parts = up_pre.reshape(2, 4, 2, 16, 896)
    results = pl.pallas_call(
        kernel,
        out_shape=held,
        in_specs=[anywhere] * 7 + [scalars] * 3,
        out_specs=[vmem] * 3,
        scratch_shapes=[
            pltpu.VMEM((16, 128, 1024), BF),
            pltpu.VMEM((16, 128, 1024), BF),
            pltpu.VMEM((16, 4, 2, 16, 1792), BF),
            pltpu.VMEM((8, 2, 2, 4, 16, 896), BF),
            pltpu.VMEM((16, 4, 2, 16, 896), BF),
            pltpu.VMEM((4, 4, 4, 32, 1024), F32),
            pltpu.VMEM((4, 4, 4, 16, 1024), F32),
            pltpu.VMEM((4, 2, 4, 32, 896), F32),
            pltpu.VMEM((2, 6, 4, 16, 896), BF),
            pltpu.VMEM((2, 6, 4, 16, 896), BF),
            pltpu.VMEM((16, 3, 4, 16, 512), BF),
            pltpu.VMEM((16, 3, 4, 16, 512), BF),
            pltpu.VMEM((16, 3, 16, 512), BF),
            pltpu.VMEM((16, 3, 16, 512), BF),
            dma((7,)),
            dma((3, 60)),
            dma((3, 4, 16)),
            dma((2, 28)),
            dma((2, 2, 2, 8)),
            dma((2, 4)),
            dma((2, 4)),
            dma((2, 6)),
            dma((2, 6)),
            dma((16, 2, 3)),
            dma((16, 2, 3)),
        ],
        compiler_params=pltpu.CompilerParams(
            collective_id=0, has_side_effects=True, vmem_limit_bytes=52 * 2**20
        ),
        cost_estimate=pl.CostEstimate(flops=flops, bytes_accessed=18 * 2**20, transcendentals=4 * 2048 * 896),
    )(inputs, grad_out, gate_parts, up_parts, w_gate, w_up, w_down, mask_gate, mask_up, mask_down)
    results = [pltpu.with_memory_space_constraint(result, pltpu.VMEM) for result in results]
    return pl.pallas_call(
        hand_over,
        out_shape=shapes,
        in_specs=[vmem] * 3,
        out_specs=[anywhere] * 4,
        scratch_shapes=[dma((4,))],
        compiler_params=pltpu.CompilerParams(vmem_limit_bytes=2 * 2**20),
        cost_estimate=pl.CostEstimate(flops=0, bytes_accessed=6 * 2**20, transcendentals=0),
    )(*results)


def solution(mesh):
    placed = (
        P("col", "row"),
        P("col", "row"),
        P("row", "col"),
        P("row", "col"),
        P("row", "col"),
        P("row", "col"),
        P("col", "row"),
        P("row", "col"),
        P("row", "col"),
        P("col", "row"),
    )
    return jax.shard_map(
        per_device,
        mesh=mesh,
        in_specs=placed,
        out_specs=(P("col", "row"), P("row", "col"), P("row", "col"), P("col", "row")),
        check_vma=False,
    )
```

```python
import jax
import jax.numpy as jnp
from jax import lax
from jax.experimental import pallas as pl
from jax.experimental.pallas import tpu as pltpu
from jax.sharding import PartitionSpec as P

MESH = pl.DeviceIdType.MESH
BF = jnp.bfloat16
F32 = jnp.float32
NT = (((1,), (1,)), ((), ()))
TN = (((0,), (0,)), ((), ()))
RELS = (2, 1, -1, 0)
GROUPS = (0, 1, -1, 2)


def m4(value):
    return lax.rem(value + 8, 4)


def coords():
    row, col = lax.axis_index("row"), lax.axis_index("col")
    return lax.div(row, 2), lax.rem(row, 2), lax.div(col, 4), lax.rem(col, 4)


def device(y, k, x, z):
    return {"row": y * 2 + k, "col": x * 4 + z}


def remote(src, dst, send, recv, to):
    return pltpu.make_async_remote_copy(
        src_ref=src, dst_ref=dst, send_sem=send, recv_sem=recv, device_id=to, device_id_type=MESH
    )


class ColGather:
    def __init__(self, full, send, recv, last, at, rows):
        self.full, self.send_sem, self.recv_sem, self.last_sem = full, send, recv, last
        self.at, self.rows = at, rows
        self.y, self.k, self.x, self.z = coords()

    def piece(self, q, c):
        return self.full.at[c, pl.ds(pl.multiple_of(q * 32 + self.at, 16), self.rows)]

    def index(self, q, a, b):
        late = lax.div(q, 2)
        return m4(self.x + a * (1 - late) + b * late) * 4 + m4(self.z + a * late + b * (1 - late))

    def send(self, q, a, b, second, d, last=False):
        c = self.index(q, a, b)
        late = lax.div(q, 2)
        along_z = late + second - 2 * late * second
        to = device(self.y, self.k, m4(self.x + d * (1 - along_z)), m4(self.z + d * along_z))
        recv = self.last_sem if last else self.recv_sem.at[q, c]
        remote(self.piece(q, c), self.piece(q, c), self.send_sem, recv, to).start()

    def recv(self, q, a, b):
        c = self.index(q, a, b)
        remote(
            self.piece(q, c),
            self.piece(q, c),
            self.send_sem,
            self.recv_sem.at[q, c],
            device(self.y, self.k, m4(self.x + 1), self.z),
        ).wait_recv()

    def each(self, body):
        def step(q, carry):
            body(q, 1 - 2 * lax.rem(q, 2))
            return carry

        lax.fori_loop(0, 4, step, 0)

    def start(self, second):
        def own(q, w):
            self.send(q, 0, 0, 0, w)
            self.send(q, 0, 0, 0, -w)

        def own_second(q, w):
            self.onward(q, 0, w)

        self.each(own_second if second else own)

    def onward(self, q, a, w):
        self.send(q, a, 0, 1, w)
        self.send(q, a, 0, 1, -w, last=True)

    def step(self, number):
        def first(q, w):
            self.recv(q, -w, 0)
            self.send(q, -w, 0, 0, w)
            self.onward(q, -w, w)

        def second(q, w):
            self.recv(q, w, 0)
            self.onward(q, w, w)

        def own_line(q, w):
            self.recv(q, 0, -w)
            self.send(q, 0, -w, 1, w, last=True)

        def far(q, w):
            self.recv(q, 2, 0)
            self.onward(q, 2, w)

        def line(q, w):
            a = (-1, 1, 2)[number - 4]
            self.recv(q, a * w, -w)
            self.send(q, a * w, -w, 1, w, last=True)

        if number < 7:
            self.each((first, second, own_line, far, line, line, line)[number])
        elif number == 10:
            self.bytes_of(32).wait_recv()

    def bytes_of(self, pieces):
        view = self.full.at[pl.ds(0, pieces * self.rows // 128)]
        to = device(self.y, self.k, m4(self.x + 1), self.z)
        return remote(view, view, self.send_sem, self.last_sem, to)

    def finish(self):
        view = self.full.at[pl.ds(0, 15), pl.ds(0, 4 * self.rows)]
        to = device(self.y, self.k, m4(self.x + 1), self.z)
        remote(view, view, self.send_sem, self.last_sem, to).wait_send()


class RowGather:
    def __init__(self, view, both, sent, send, recv, cross_recv):
        self.view, self.both, self.sent = view, both, sent
        self.send_sem, self.recv_sem, self.cross_sem = send, recv, cross_recv
        self.y, self.k, self.x, self.z = coords()

    def row(self, dy, sibling=False):
        return m4(self.y + dy) * 2 + (1 - self.k if sibling else self.k)

    def sibling(self):
        return device(self.y, 1 - self.k, self.x, self.z)

    def ring_copy(self, p, h, r, to):
        view = self.view(r, p, h)
        return remote(view, view, self.send_sem.at[p], self.recv_sem.at[p, h, r], to)

    def ring(self, p, h, dy, d):
        self.ring_copy(p, h, self.row(dy), device(m4(self.y + d), self.k, self.x, self.z)).start()

    def cross(self, p, h, dy):
        r = self.row(dy)
        view = self.view(r, p, h)
        remote(view, view, self.send_sem.at[p], self.cross_sem.at[p, r], self.sibling()).start()

    def recv(self, p, h, dy):
        self.ring_copy(p, h, self.row(dy), self.sibling()).wait_recv()

    def start(self, p, second):
        self.ring(p, second, 0, 1)
        self.ring(p, 1 - second, 0, -1)
        self.cross(p, second, 0)

    def near(self, p):
        for h in (0, 1):
            w = 1 - 2 * h
            self.recv(p, h, -w)
            self.ring(p, h, -w, w)
            self.cross(p, h, -w)

    def other(self, p):
        for h in (0, 1):
            w = 1 - 2 * h
            self.recv(p, h, w)
            self.cross(p, h, w)

    def far(self, p):
        for h in (0, 1):
            self.recv(p, h, 2)
            self.cross(p, h, 2)

    def from_sibling(self, p, dy):
        r = self.row(dy, True)
        view = self.both(r, p)
        remote(view, view, self.send_sem.at[p], self.cross_sem.at[p, r], self.sibling()).wait_recv()

    def finish(self, p):
        view = self.sent(p)
        remote(view, view, self.send_sem.at[p], self.cross_sem.at[p, 0], self.sibling()).wait_send()


def kernel(
    x_in, dy_in, g_in, u_in, wg_in, wu_in, wd_in, mg_in, mu_in, md_in,
    gi, gw, gd,
    dy, xx, gu, hd, act, hp, pa, rb, ys, yr, s1, r1, s2, r2,
    mg, mu, md, lsem, col_s, col_r, col_l, row_s, row_r, row_c, sib_s, sib_r, ring_s, ring_r, gs, gr,
):
    y, k, x, z = coords()
    me_col, me_row = x * 4 + z, y * 2 + k
    sibling = device(y, 1 - k, x, z)
    up_y, down_y = device(m4(y + 1), k, x, z), device(m4(y - 1), k, x, z)

    two, left_half, right_half = pl.ds(2 * me_row, 2), pl.ds(0, 896), pl.ds(896, 896)
    local = [
        pltpu.make_async_copy(dy_in, dy.at[me_col], lsem.at[0]),
        pltpu.make_async_copy(g_in, gu.at[two, :, :, :, left_half], lsem.at[1]),
        pltpu.make_async_copy(u_in, gu.at[two, :, :, :, right_half], lsem.at[2]),
        pltpu.make_async_copy(wd_in, gd, lsem.at[3]),
        pltpu.make_async_copy(x_in, xx.at[me_col], lsem.at[4]),
        pltpu.make_async_copy(wg_in, gw.at[:, left_half], lsem.at[5]),
        pltpu.make_async_copy(wu_in, gw.at[:, right_half], lsem.at[6]),
        pltpu.make_async_copy(md_in, md, lsem.at[7]),
        pltpu.make_async_copy(mg_in, mg, lsem.at[8]),
        pltpu.make_async_copy(mu_in, mu, lsem.at[9]),
    ]
    for copy in local:
        copy.start()

    barrier = pltpu.get_barrier_semaphore()
    for to in (
        device(y, k, m4(x + 1), z),
        device(y, k, m4(x - 1), z),
        device(y, k, x, m4(z + 1)),
        device(y, k, x, m4(z - 1)),
        device(y, k, m4(x + 2), z),
        device(y, k, x, m4(z + 2)),
        up_y,
        down_y,
        sibling,
    ):
        pl.semaphore_signal(barrier, inc=1, device_id=to, device_id_type=MESH)
    pl.semaphore_wait(barrier, 9)

    dy_gathers = [ColGather(dy, col_s.at[p], col_r.at[p], col_l.at[p], 16 * p, 16) for p in range(2)]
    x_gather = ColGather(xx, col_s.at[2], col_r.at[2], col_l.at[2], 0, 32)
    g_gather = RowGather(
        lambda r, p, h: gu.at[2 * r + h, :, p],
        lambda r, p: gu.at[pl.ds(2 * r, 2), :, p],
        lambda p: gu.at[pl.ds(0, 14), :, p],
        row_s.at[0],
        row_r.at[0],
        row_c.at[0],
    )
    h_gather = RowGather(
        lambda r, p, h: hd.at[r, p, h],
        lambda r, p: hd.at[r, p],
        lambda p: hd.at[pl.ds(0, 7), p],
        row_s.at[1],
        row_r.at[1],
        row_c.at[1],
    )

    def apply_mask(w, mask, rows, columns, first=0):
        def line(i, carry):
            here = pl.ds(pl.multiple_of(i * 128, 128), 128)
            for j in range(columns):
                keep = mask[i, j].astype(F32)
                block = w[here, first + j * 128 : first + (j + 1) * 128].astype(F32)
                w[here, first + j * 128 : first + (j + 1) * 128] = (block * keep).astype(BF)
            return carry

        lax.fori_loop(0, rows, line, 0)

    def across(p, slot):
        there, rows = pl.ds(2 * (1 - k), 2), pl.ds(16 * p, 16)
        return remote(
            hp.at[slot, there, :, rows, pl.ds(0, 896)],
            rb.at[slot, :, :, rows],
            sib_s.at[p, slot],
            sib_r.at[p, slot],
            sibling,
        )

    def partial(p, slot):
        j = m4(y + RELS[slot])
        rows = pl.ds(pl.multiple_of(j * 32 + p * 16, 16), 16)
        left = dy[:, rows, :].reshape(256, 1024)
        product = lax.dot_general(left, gd[...], NT, preferred_element_type=F32)
        hp[slot, :, :, p * 16 : p * 16 + 16, 0:896] = product.reshape(4, 4, 16, 896)
        across(p, slot).start()

    def total(p, slot, h, i):
        rows = pl.ds(p * 16, 16)
        return hp[slot, 2 * k + h, i, rows, 0:896] + rb[slot, h, i, rows]

    def ring_copy(p, n):
        to = up_y if n % 2 == 0 else down_y
        return remote(ys.at[p, n], yr.at[p, n], ring_s.at[p], ring_r.at[p, n], to)

    def ring_sent(p):
        remote(ys.at[p], yr.at[p], ring_s.at[p], ring_r.at[p, 0], up_y).wait_send()

    def pack(p, n, slot, h, with_recv=None):
        if with_recv is not None:
            ring_copy(p, with_recv).wait_recv()

        def one(i, carry):
            value = total(p, slot, h, i)
            if with_recv is not None:
                value = value + yr[p, with_recv, i].astype(F32)
            ys[p, n, i] = value.astype(BF)
            return carry

        lax.fori_loop(0, 4, one, 0)
        ring_copy(p, n).start()

    def pack_far(p):
        pack(p, 0, 0, 0)
        pack(p, 1, 0, 1)

    def pack_near(p):
        pack(p, 2, 1, 1)
        pack(p, 3, 2, 0)

    def pack_sum(p):
        pack(p, 4, 1, 0, 0)
        pack(p, 5, 2, 1, 1)

    def finish_hidden(p):
        for h, first, second in ((0, 3, 4), (1, 2, 5)):
            ring_copy(p, first).wait_recv()
            ring_copy(p, second).wait_recv()

            def one(i, carry, h=h, first=first, second=second):
                value = total(p, 3, h, i) + yr[p, first, i].astype(F32) + yr[p, second, i].astype(F32)
                hd[me_row, p, h, i] = value.astype(BF)
                return carry

            lax.fori_loop(0, 4, one, 0)
        h_gather.start(p, 0)
        h_gather.start(p, 1)

    def activation(p):
        def one(c, carry):
            for j in range(4):
                gated = gu[c, j, p, :, 0:896].astype(F32)
                upper = gu[c, j, p, :, 896:1792].astype(F32)
                act[c, j, p] = (gated * jax.nn.sigmoid(gated) * upper).astype(BF)
            return carry

        lax.fori_loop(0, 16, one, 0)

    def keep_blocks(product, mask, out, i, rows, columns, first=0):
        for p in range(rows // 128):
            for q in range(columns // 128):
                keep = mask[i * 2 + p, q].astype(F32)
                at = first + q * 128
                block = product[p * 128 : (p + 1) * 128, at : at + 128]
                out[i * 256 + p * 128 : i * 256 + (p + 1) * 128, at : at + 128] = (block * keep).astype(BF)

    def down_tile(i):
        rows = 256 if i < 3 else 128
        a = act[:, :, :, :, i * 256 : i * 256 + rows].reshape(2048, rows)
        b = dy[...].reshape(2048, 1024)
        product = lax.dot_general(a, b, TN, preferred_element_type=F32)
        keep_blocks(product, md, gd, i, rows, 1024)

    def pair_tile(i):
        a = xx[:, :, i * 256 : (i + 1) * 256].reshape(2048, 256)
        b = gu[...].reshape(2048, 1792)
        product = lax.dot_general(a, b, TN, preferred_element_type=F32)
        keep_blocks(product, mg, gw, i, 256, 896)
        keep_blocks(product, mu, gw, i, 256, 896, 896)

    offsets = (2, 1, -1)

    def group_copy(p, n, t, stage_at, i):
        d = offsets[i]
        if t == stage_at:
            to = device(y, k, x, m4(z + d))
        else:
            to = device(y, k, m4(x + d), z)
        at = p * 8 + n * 2 + t
        src, dst = (s1, r1) if stage_at == 0 else (s2, r2)
        return remote(src.at[at, i], dst.at[at, i], gs.at[stage_at], gr.at[p * 4 + n, stage_at], to)

    def group_wait(p, n, stage_at):
        both = pl.ds(p * 8 + n * 2, 2)
        src, dst = (s1, r1) if stage_at == 0 else (s2, r2)
        remote(src.at[both], dst.at[both], gs.at[stage_at], gr.at[p * 4 + n, stage_at], sibling).wait_recv()

    def columns(t):
        return pl.ds(t * 512, 512)

    def partials(p):
        return pa if p == 0 else hp

    def group_partial(p, n):
        j = m4(y + GROUPS[n])

        def one(c, carry):
            gated = gu[c, j, p, :, 0:896].astype(F32)
            upper = gu[c, j, p, :, 896:1792].astype(F32)
            hidden = hd[2 * j + lax.div(c, 8), p, lax.rem(lax.div(c, 4), 2), lax.rem(c, 4)].astype(F32)
            sigma = jax.nn.sigmoid(gated)
            gu[c, j, p, :, 0:896] = (hidden * upper * sigma * (1.0 + gated * (1.0 - sigma))).astype(BF)
            gu[c, j, p, :, 896:1792] = (hidden * gated * sigma).astype(BF)
            return carry

        lax.fori_loop(0, 16, one, 0)
        product = lax.dot_general(gu[:, j, p].reshape(256, 1792), gw[...], NT, preferred_element_type=F32)
        partials(p)[n, :, :, 0:16, :] = product.reshape(4, 4, 16, 1024)
        for i, d in enumerate(offsets):
            s1[p * 8 + n * 2, i] = partials(p)[n, :, m4(z + d), 0:16, columns(0)].astype(BF)
            group_copy(p, n, 0, 0, i).start()
            s1[p * 8 + n * 2 + 1, i] = partials(p)[n, m4(x + d), :, 0:16, columns(1)].astype(BF)
            group_copy(p, n, 1, 0, i).start()

    def line_total(p, n, t, d):
        at = p * 8 + n * 2 + t
        if t == 0:
            to = m4(x + d)
            own = partials(p)[n, to, z, 0:16, columns(t)]
        else:
            to = m4(z + d)
            own = partials(p)[n, x, to, 0:16, columns(t)]
        for i in range(3):
            own = own + r1[at, i, to].astype(F32)
        return own

    def group_second(p, n):
        group_wait(p, n, 0)
        for i, d in enumerate(offsets):
            for t in range(2):
                s2[p * 8 + n * 2 + t, i] = line_total(p, n, t, d).astype(BF)
                group_copy(p, n, t, 1, i).start()

    def group_last(p, n):
        j = m4(y + GROUPS[n])
        rows = pl.ds(pl.multiple_of(j * 32 + p * 16, 16), 16)
        group_wait(p, n, 1)
        for t in range(2):
            value = line_total(p, n, t, 0)
            for i in range(3):
                value = value + r2[p * 8 + n * 2 + t, i].astype(F32)
            gi[rows, columns(t)] = value.astype(BF)

    local[0].wait()
    dy_gathers[0].start(0)
    dy_gathers[0].start(1)
    local[1].wait()
    local[2].wait()
    g_gather.start(0, 0)
    g_gather.start(0, 1)
    g_gather.start(1, 0)
    g_gather.start(1, 1)
    dy_gathers[0].step(0)
    dy_gathers[0].step(1)
    dy_gathers[1].start(0)
    dy_gathers[1].start(1)
    local[4].wait()
    x_gather.start(0)
    dy_gathers[0].step(2)
    g_gather.near(0)
    dy_gathers[0].step(3)
    dy_gathers[0].step(4)
    dy_gathers[0].step(5)
    local[3].wait()
    local[7].wait()
    apply_mask(gd, md, 7, 8)
    local[5].wait()
    local[8].wait()
    apply_mask(gw, mg, 8, 7)
    local[6].wait()
    local[9].wait()
    apply_mask(gw, mu, 8, 7, 896)
    dy_gathers[1].step(0)
    dy_gathers[1].step(1)
    g_gather.other(0)
    dy_gathers[1].step(2)
    g_gather.near(1)
    dy_gathers[0].step(6)
    dy_gathers[0].step(7)
    dy_gathers[0].step(8)
    dy_gathers[0].step(9)
    dy_gathers[1].step(3)
    x_gather.start(1)
    dy_gathers[1].step(4)
    g_gather.other(1)
    dy_gathers[1].step(5)
    dy_gathers[0].step(10)
    partial(0, 0)
    partial(0, 1)
    dy_gathers[1].step(6)
    dy_gathers[1].step(7)
    partial(0, 2)
    across(0, 0).wait_recv()
    pack_far(0)
    partial(0, 3)
    g_gather.far(0)
    x_gather.step(0)
    x_gather.step(1)
    across(0, 1).wait_recv()
    across(0, 2).wait_recv()
    pack_near(0)
    x_gather.step(2)
    dy_gathers[1].step(8)
    dy_gathers[1].step(9)
    for offset in (0, 1, -1, 2):
        g_gather.from_sibling(0, offset)
    activation(0)
    g_gather.finish(0)
    dy_gathers[1].step(10)
    partial(1, 0)
    partial(1, 1)
    partial(1, 2)
    partial(1, 3)
    across(1, 0).wait_recv()
    pack_far(1)
    g_gather.far(1)
    pack_sum(0)
    x_gather.step(3)
    x_gather.step(4)
    across(1, 1).wait_recv()
    across(1, 2).wait_recv()
    pack_near(1)
    for offset in (0, 1, -1, 2):
        g_gather.from_sibling(1, offset)
    activation(1)
    g_gather.finish(1)
    down_tile(2)
    x_gather.step(5)
    down_tile(0)
    pack_sum(1)
    down_tile(1)
    x_gather.step(6)
    across(0, 3).wait_recv()
    finish_hidden(0)
    x_gather.step(7)
    down_tile(3)
    x_gather.step(8)
    h_gather.from_sibling(0, 0)
    group_partial(0, 0)
    x_gather.step(9)
    x_gather.step(10)
    across(1, 3).wait_recv()
    finish_hidden(1)
    for p in range(2):
        for slot in range(4):
            across(p, slot).wait_send()
    h_gather.from_sibling(1, 0)
    group_partial(1, 0)
    h_gather.near(0)
    group_second(0, 0)
    h_gather.other(0)
    h_gather.from_sibling(0, 1)
    group_partial(0, 1)
    h_gather.near(1)
    h_gather.from_sibling(0, -1)
    group_partial(0, 2)
    h_gather.other(1)
    group_last(0, 0)
    group_second(1, 0)
    h_gather.from_sibling(1, 1)
    group_partial(1, 1)
    h_gather.far(0)
    group_second(0, 1)
    h_gather.from_sibling(1, -1)
    group_partial(1, 2)
    h_gather.far(1)
    h_gather.from_sibling(0, 2)
    group_partial(0, 3)
    h_gather.from_sibling(1, 2)
    group_partial(1, 3)
    group_second(1, 1)
    pair_tile(0)
    group_second(1, 2)
    pair_tile(2)
    group_second(0, 3)
    group_second(0, 2)
    pair_tile(1)
    group_second(1, 3)
    group_last(1, 1)
    group_last(0, 1)
    group_last(1, 0)
    pair_tile(3)
    group_last(1, 2)
    group_last(0, 2)
    group_last(0, 3)
    group_last(1, 3)
    ring_sent(0)
    ring_sent(1)

    dy_gathers[0].finish()
    dy_gathers[1].finish()
    x_gather.finish()
    h_gather.finish(0)
    h_gather.finish(1)

    remote(s1, r1, gs.at[0], gr.at[0, 0], sibling).wait_send()
    remote(s2, r2, gs.at[1], gr.at[0, 1], sibling).wait_send()


def hand_over(gi, gw, gd, gi_out, gg_out, gu_out, gd_out, sems):
    copies = [
        (gw.at[:, pl.ds(0, 896)], gg_out),
        (gw.at[:, pl.ds(896, 896)], gu_out),
        (gd, gd_out),
        (gi, gi_out),
    ]
    copies = [pltpu.make_async_copy(src, dst, sems.at[n]) for n, (src, dst) in enumerate(copies)]
    for copy in copies:
        copy.start()
    for copy in copies:
        copy.wait()


def per_device(
    inputs, grad_out, gate_pre, up_pre, w_gate, w_up, w_down, mask_gate, mask_up, mask_down
):
    anywhere = pl.BlockSpec(memory_space=pl.ANY)
    vmem = pl.BlockSpec(memory_space=pltpu.VMEM)
    held = [pltpu.VMEM((128, 1024), BF), pltpu.VMEM((1024, 1792), BF), pltpu.VMEM((896, 1024), BF)]
    dma = pltpu.SemaphoreType.DMA
    flops = 2 * 2048 * 1024 * 896 * 6
    shapes = [
        jax.ShapeDtypeStruct((128, 1024), BF),
        jax.ShapeDtypeStruct((1024, 896), BF),
        jax.ShapeDtypeStruct((1024, 896), BF),
        jax.ShapeDtypeStruct((896, 1024), BF),
    ]
    gate_parts = gate_pre.reshape(2, 4, 2, 16, 896)
    up_parts = up_pre.reshape(2, 4, 2, 16, 896)
    results = pl.pallas_call(
        kernel,
        out_shape=held,
        in_specs=[anywhere] * 10,
        out_specs=[vmem] * 3,
        scratch_shapes=[
            pltpu.VMEM((16, 128, 1024), BF),
            pltpu.VMEM((16, 128, 1024), BF),
            pltpu.VMEM((16, 4, 2, 16, 1792), BF),
            pltpu.VMEM((8, 2, 2, 4, 16, 896), BF),
            pltpu.VMEM((16, 4, 2, 16, 896), BF),
            pltpu.VMEM((4, 4, 4, 32, 1024), F32),
            pltpu.VMEM((4, 4, 4, 16, 1024), F32),
            pltpu.VMEM((4, 2, 4, 32, 896), F32),
            pltpu.VMEM((2, 6, 4, 16, 896), BF),
            pltpu.VMEM((2, 6, 4, 16, 896), BF),
            pltpu.VMEM((16, 3, 4, 16, 512), BF),
            pltpu.VMEM((16, 3, 4, 16, 512), BF),
            pltpu.VMEM((16, 3, 16, 512), BF),
            pltpu.VMEM((16, 3, 16, 512), BF),
            pltpu.SMEM((8, 7), jnp.int32),
            pltpu.SMEM((8, 7), jnp.int32),
            pltpu.SMEM((7, 8), jnp.int32),
            dma((10,)),
            dma((3,)),
            dma((3, 4, 16)),
            dma((3,)),
            dma((2, 2)),
            dma((2, 2, 2, 8)),
            dma((2, 2, 8)),
            dma((2, 4)),
            dma((2, 4)),
            dma((2,)),
            dma((2, 6)),
            dma((2,)),
            dma((8, 2)),
        ],
        compiler_params=pltpu.CompilerParams(
            collective_id=0, has_side_effects=True, vmem_limit_bytes=52 * 2**20
        ),
        cost_estimate=pl.CostEstimate(flops=flops, bytes_accessed=18 * 2**20, transcendentals=4 * 2048 * 896),
    )(inputs, grad_out, gate_parts, up_parts, w_gate, w_up, w_down, mask_gate, mask_up, mask_down)
    results = [pltpu.with_memory_space_constraint(result, pltpu.VMEM) for result in results]
    return pl.pallas_call(
        hand_over,
        out_shape=shapes,
        in_specs=[vmem] * 3,
        out_specs=[anywhere] * 4,
        scratch_shapes=[dma((4,))],
        compiler_params=pltpu.CompilerParams(vmem_limit_bytes=2 * 2**20),
        cost_estimate=pl.CostEstimate(flops=0, bytes_accessed=6 * 2**20, transcendentals=0),
    )(*results)


def solution(mesh):
    placed = (
        P("col", "row"),
        P("col", "row"),
        P("row", "col"),
        P("row", "col"),
        P("row", "col"),
        P("row", "col"),
        P("col", "row"),
        P("row", "col"),
        P("row", "col"),
        P("col", "row"),
    )
    return jax.shard_map(
        per_device,
        mesh=mesh,
        in_specs=placed,
        out_specs=(P("col", "row"), P("row", "col"), P("row", "col"), P("col", "row")),
        check_vma=False,
    )
```
